512 devices in a mesh: grp: 16 (over y, core), seq: 32 (over z, x).
Axes of the slice: x: 4, y: 8, z: 8, core: 2. Of those that a mesh axis runs over, the one named last changes fastest.
Arguments:
- conv_input: bfloat16 [65536, 9216], P(('grp', 'seq')), may hold values from -6 to 6
- conv_weight: float32 [4, 9216], replicated, may hold values from -3 to 3
- step_raw: float32 [65536, 128], P(('grp', 'seq')), may hold values from -30 to 1
- decay_log: float32 [128], replicated, may hold values from -12 to 6
- skip_gain: float32 [128], replicated, may hold values from 0.5 to 2
Outputs:
- mixer_output: bfloat16 [65536, 8192], P(('grp', 'seq'))
The draws below stay inside these ranges and needn't reach their ends.
All inputs are finite; a program needn't handle non-finite values.
Results may differ from the reference program's by a relative error of at most 0.005.
The reference program's roundings to bfloat16 on the way (of `values`, `writers`, `readers`, `scores`, `weighted` and `entering_low`) count: a program that leaves them out, or rounds other values in their place, can miss the bound.
Values may be sent and summed in bfloat16 or wider, within the bound.
No kernel may reach another device: no remote copies, remote signals or barrier semaphores. Data moves between devices by JAX's collectives and lax.ppermute only.
A program may use at most 64 MiB of HBM per device.

```python
import jax
import jax.numpy as jnp
from jax import lax

HEADS = 128
HEAD_DIM = 64
STATE = 128
GROUPS = 4
KERNEL = 4
TOK_DEV = 128
SEQLEN = 65536
CHANNELS = 9216


def head_law(key):
    chooser = jax.random.uniform(jax.random.fold_in(key, 11), (HEADS,))
    fraction = 0.5
    quick_heads = chooser < fraction
    spread_draw = jax.random.uniform(jax.random.fold_in(key, 12), (HEADS,))
    quick_rate = jnp.exp(jnp.log(1.0 / 50.0) + spread_draw * jnp.log(50.0 / 30.0))
    slow_total = jnp.exp(jnp.log(0.3) + spread_draw * jnp.log(5.0))
    rate_token = jnp.where(quick_heads, quick_rate, slow_total / SEQLEN)
    memory = jnp.where(quick_heads, 1.0 / quick_rate, SEQLEN * 1.0)
    base_step = 1.0 / jnp.sqrt(STATE * memory)
    return (rate_token, base_step)


def draw_decay_log(key, part):
    rate_token, base_step = head_law(key)
    return jnp.log(rate_token / base_step).astype(jnp.float32)


def draw_step_raw(key, part):
    rate_token, base_step = head_law(key)
    nblocks = SEQLEN // TOK_DEV
    roughness = jnp.exp(jax.random.uniform(jax.random.fold_in(key, 13), (nblocks, TOK_DEV, HEADS), minval=-1.2, maxval=1.2))
    block_factor = jnp.exp(jax.random.uniform(jax.random.fold_in(key, 14), (nblocks, 1, 1), minval=-0.7, maxval=0.7))
    step_size = (base_step * roughness * block_factor).reshape(SEQLEN, HEADS)
    return jnp.log(jnp.expm1(step_size)).astype(jnp.float32)


def levels(own_key, extent, pieces, smallest, top_value):
    level, own = 1.0, jax.random.fold_in(own_key, 6)
    for axis_at, parts in pieces:
        steps = jnp.exp(jax.random.uniform(jax.random.fold_in(own, axis_at), (parts,), jnp.float32, smallest / len(pieces), top_value / len(pieces)))
        level = level * jnp.repeat(steps, extent[axis_at] // parts).reshape([-1 if axis == axis_at else 1 for axis in range(len(extent))])
    return level


def noise(stream_key, extent, spread, most, split=(), held_as=jnp.bfloat16):
    entries = spread * jax.random.normal(stream_key, extent, jnp.float32)
    if split:
        entries = entries * levels(stream_key, extent, split, -0.22, 0.18)
    return jnp.clip(entries, -most, most).astype(held_as)


def setup_inputs(seed: int = 0) -> dict:
    arg_keys = jax.random.split(jax.random.key(seed), 6)
    conv_input = noise(arg_keys[0], (SEQLEN, CHANNELS), 1.0, 6.0, ((0, 512),))
    conv_weight = noise(arg_keys[1], (KERNEL, CHANNELS), KERNEL ** -0.5, 3.0, (), jnp.float32)
    step_raw = draw_step_raw(jax.random.fold_in(arg_keys[5], 71), 0)
    decay_log = draw_decay_log(jax.random.fold_in(arg_keys[5], 71), 0)
    skip_gain = jnp.clip(jax.random.uniform(arg_keys[4], (HEADS,), jnp.float32, 0.5, 2.0), 0.5, 2.0)
    return {"conv_input": conv_input, "conv_weight": conv_weight, "step_raw": step_raw, "decay_log": decay_log, "skip_gain": skip_gain}


def reference(conv_input, conv_weight, step_raw, decay_log, skip_gain):
    per_group = HEADS // GROUPS
    head_cols = HEADS * HEAD_DIM
    group_cols = GROUPS * STATE
    nblocks = SEQLEN // TOK_DEV
    block_rows = conv_input.reshape(nblocks, TOK_DEV, CHANNELS)
    block_steps = step_raw.reshape(nblocks, TOK_DEV, HEADS)
    coeff = -jnp.exp(decay_log)

    def advance(carry, item):
        state, tail = carry
        rows_now, steps_now = item
        widened = jnp.concatenate([tail, rows_now], 0).astype(jnp.float32)
        convolved = jnp.zeros((TOK_DEV, CHANNELS), jnp.float32)
        for tap in range(KERNEL):
            convolved = convolved + widened[tap:tap + TOK_DEV] * conv_weight[tap]
        values = convolved[:, :head_cols].astype(jnp.bfloat16).reshape(TOK_DEV, GROUPS, per_group, HEAD_DIM)
        writers = convolved[:, head_cols:head_cols + group_cols].astype(jnp.bfloat16).reshape(TOK_DEV, GROUPS, STATE)
        readers = convolved[:, head_cols + group_cols:].astype(jnp.bfloat16).reshape(TOK_DEV, GROUPS, STATE)
        values_f = values.astype(jnp.float32)
        writers_f = writers.astype(jnp.float32)
        readers_f = readers.astype(jnp.float32)
        step_size = jax.nn.softplus(steps_now)
        cumulative = jnp.cumsum(coeff * step_size, axis=0)
        affinity = jnp.einsum('tgn,ugn->gtu', readers_f, writers_f)
        cum_heads = cumulative.T.reshape(GROUPS, per_group, TOK_DEV)
        differences = cum_heads[:, :, :, None] - cum_heads[:, :, None, :]
        positions = jnp.arange(TOK_DEV, dtype=jnp.int32)
        causal = positions[:, None] >= positions[None, :]
        weights = jnp.exp(jnp.where(causal, differences, -jnp.inf)) * step_size.T.reshape(GROUPS, per_group, 1, TOK_DEV)
        scores = (weights * affinity[:, None]).astype(jnp.bfloat16).astype(jnp.float32)
        local_part = jnp.einsum('gktu,ugkp->tgkp', scores, values_f)
        last = cumulative[TOK_DEV - 1]
        factor = (jnp.exp(last - cumulative) * step_size).reshape(TOK_DEV, GROUPS, per_group, 1)
        weighted = (values_f * factor).astype(jnp.bfloat16).astype(jnp.float32)
        block_state = jnp.einsum('ugkp,ugn->gkpn', weighted, writers_f)
        block_decay = jnp.exp(last).reshape(GROUPS, per_group)
        entering_low = state.astype(jnp.bfloat16).astype(jnp.float32)
        carried_part = jnp.einsum('tgn,gkpn->tgkp', readers_f, entering_low) * jnp.exp(cumulative).reshape(TOK_DEV, GROUPS, per_group, 1)
        result = (local_part + carried_part) + skip_gain.reshape(GROUPS, per_group, 1) * values_f
        new_state = block_decay[:, :, None, None] * state + block_state
        new_tail = rows_now[TOK_DEV - KERNEL + 1:]
        return (new_state, new_tail), result.reshape(TOK_DEV, head_cols).astype(jnp.bfloat16)

    start_state = jnp.zeros((GROUPS, per_group, HEAD_DIM, STATE), jnp.float32)
    start_tail = jnp.zeros((KERNEL - 1, CHANNELS), jnp.bfloat16)
    ignored, outputs = lax.scan(advance, (start_state, start_tail), (block_rows, block_steps))
    return outputs.reshape(SEQLEN, head_cols)
```

```python
import functools

import jax
import jax.numpy as jnp
from jax import lax
from jax.experimental import pallas as pl
from jax.experimental.pallas import tpu as pltpu
from jax.sharding import Mesh, PartitionSpec as P

HEADS = 128
HEAD_DIM = 64
STATE = 128
GROUPS = 4
KERNEL = 4
TOK = 128
PER = HEADS // GROUPS
GCOLS = PER * HEAD_DIM
NB = GCOLS // 128
HCOLS = HEADS * HEAD_DIM
ROWS = NB * STATE
PAY = ROWS + 3 * NB
SHARES = 64
SROWS = ROWS // SHARES
TROWS = SROWS + 8
NX, NY, NZ = 4, 8, 8
F32 = jnp.float32
BF16 = jnp.bfloat16
LIMIT = 32 * 1024 * 1024
AXES = ("y", "core", "z", "x")


def params():
    return pltpu.CompilerParams(vmem_limit_bytes=LIMIT)


def three(v):
    hi = v.astype(BF16).astype(F32)
    mid = (v - hi).astype(BF16).astype(F32)
    low = (v - hi - mid).astype(BF16).astype(F32)
    return hi, mid, low


def lanes_of(per_head, base, block, rows):
    lane = lax.broadcasted_iota(jnp.int32, (rows, 128), 1)
    pick = base + 2 * block + lane // HEAD_DIM
    return jnp.take_along_axis(per_head, pick, axis=1)


def prep_kernel(raw_ref, log_ref, cum_ref, factor_ref, growth_ref, cum_t_ref, step_t_ref, decay_ref):
    raw = raw_ref[...]
    step = jnp.maximum(raw, 0.0) + jnp.log1p(jnp.exp(-jnp.abs(raw)))
    cum = -jnp.exp(log_ref[...]) * step
    row = lax.broadcasted_iota(jnp.int32, (TOK, HEADS), 0)
    shift = 1
    while shift < TOK:
        cum = cum + jnp.where(row >= shift, pltpu.roll(cum, shift, 0), 0.0)
        shift *= 2
    last = cum[TOK - 1 :, :]
    cum_ref[...] = cum
    factor_ref[...] = jnp.exp(last - cum) * step
    growth_ref[...] = jnp.exp(cum)
    cum_t_ref[...] = cum.T
    step_t_ref[...] = step.T
    decay_ref[...] = jnp.broadcast_to(jnp.exp(last), (8, HEADS))


def prep(step_raw, decay_log):
    square = jax.ShapeDtypeStruct((TOK, HEADS), F32)
    return pl.pallas_call(
        prep_kernel,
        out_shape=[square] * 5 + [jax.ShapeDtypeStruct((8, HEADS), F32)],
        compiler_params=params(),
    )(step_raw, decay_log.reshape(1, HEADS))


def convolve(x_ref, edge_ref, w_ref, lo):
    cols = slice(lo, lo + 128)
    x = x_ref[:, cols].astype(F32)
    edge = edge_ref[:, cols].astype(F32)
    wide = jnp.concatenate([jnp.zeros((8 - KERNEL + 1, 128), F32), edge, x], 0)
    out = None
    for tap in range(KERNEL):
        at = 8 - KERNEL + 1 + tap
        term = wide[at : at + TOK] * w_ref[tap : tap + 1, cols]
        out = term if out is None else out + term
    return out.astype(BF16)


CHUNKS = 4
CB = NB // CHUNKS


def state_kernel(
    pick_ref, xv, xw, xr, ev, ew, er, wv, ww, wr, factor_ref, decay_ref,
    pay_ref, val_ref, wri_ref, rea_ref, wt_ref,
):
    step = pl.program_id(0)
    base = pick_ref[0] * PER

    @pl.when(step == 0)
    def _():
        writers = convolve(xw, ew, ww, 0)
        wri_ref[...] = writers
        wt_ref[...] = writers.astype(F32).T.astype(BF16)
        rea_ref[...] = convolve(xr, er, wr, 0)
        rows = [lanes_of(decay_ref[...], base, b, 8)[:1] for b in range(NB)]
        for at, term in enumerate(three(jnp.concatenate(rows, 0))):
            pay_ref[ROWS + at * NB : ROWS + (at + 1) * NB] = term.astype(BF16)

    factor = factor_ref[...]
    for pair in range(CB // 2):
        weighted = []
        for half in range(2):
            b = 2 * pair + half
            value = convolve(xv, ev, wv, b * 128)
            val_ref[:, b * 128 : (b + 1) * 128] = value
            fac = lanes_of(factor, base, step * CB + b, TOK)
            weighted.append((value.astype(F32) * fac).astype(BF16))
        state = jnp.dot(wt_ref[...], jnp.concatenate(weighted, 1), preferred_element_type=F32)
        for half in range(2):
            at = pl.multiple_of((step * CB + 2 * pair + half) * STATE, STATE)
            pay_ref[pl.ds(at, STATE)] = state[:, half * 128 : (half + 1) * 128].astype(BF16)


def states(pick, conv_input, edge, conv_weight, factor, decay):
    width = CB * 128
    head_blocks = HCOLS // 128

    def three_of(rows):
        return [
            pl.BlockSpec((rows, width), lambda i, p: (0, p[0] * CHUNKS + i)),
            pl.BlockSpec((rows, 128), lambda i, p: (0, head_blocks + p[0])),
            pl.BlockSpec((rows, 128), lambda i, p: (0, head_blocks + GROUPS + p[0])),
        ]

    whole = lambda shape: pl.BlockSpec(shape, lambda i, p: (0, 0))
    return pl.pallas_call(
        state_kernel,
        grid_spec=pltpu.PrefetchScalarGridSpec(
            num_scalar_prefetch=1,
            grid=(CHUNKS,),
            in_specs=three_of(TOK) + three_of(KERNEL - 1) + three_of(KERNEL)
            + [whole((TOK, HEADS)), whole((8, HEADS))],
            out_specs=[
                whole((PAY, 128)),
                pl.BlockSpec((TOK, width), lambda i, p: (0, i)),
                whole((TOK, STATE)),
                whole((TOK, STATE)),
            ],
            scratch_shapes=[pltpu.VMEM((STATE, TOK), BF16)],
        ),
        out_shape=[
            jax.ShapeDtypeStruct((PAY, 128), BF16),
            jax.ShapeDtypeStruct((TOK, GCOLS), BF16),
            jax.ShapeDtypeStruct((TOK, STATE), BF16),
            jax.ShapeDtypeStruct((TOK, STATE), BF16),
        ],
        compiler_params=params(),
        cost_estimate=pl.CostEstimate(flops=10**8, bytes_accessed=3 * 10**6, transcendentals=0),
    )(pick, *([conv_input] * 3), *([edge] * 3), *([conv_weight] * 3), factor, decay)


def local_kernel(pick_ref, val_ref, wri_ref, rea_ref, cum_ref, cum_t_ref, step_t_ref, gain_ref, out_ref):
    base = pick_ref[0] * PER
    affinity = lax.dot_general(
        rea_ref[...], wri_ref[...], (((1,), (1,)), ((), ())), preferred_element_type=F32
    )
    cum = cum_ref[...]
    gain = jnp.broadcast_to(gain_ref[...], (8, HEADS))
    row = lax.broadcasted_iota(jnp.int32, (TOK, TOK), 0)
    col = lax.broadcasted_iota(jnp.int32, (TOK, TOK), 1)
    causal = row >= col
    first = col < HEAD_DIM
    for b in range(NB):
        scores = []
        for half in range(2):
            h = 2 * b + half
            at = jnp.take_along_axis(cum, jnp.full((TOK, TOK), base + h, jnp.int32), axis=1)
            span = jnp.where(causal, at - cum_t_ref[h : h + 1], -1e30)
            weight = jnp.exp(span) * step_t_ref[h : h + 1]
            scores.append((weight * affinity).astype(BF16))
        value = val_ref[:, b * 128 : (b + 1) * 128]
        zero = jnp.zeros_like(value)
        apart = jnp.concatenate([jnp.where(first, value, zero), jnp.where(first, zero, value)], 0)
        part = jnp.dot(jnp.concatenate(scores, 1), apart, preferred_element_type=F32)
        skip = lanes_of(gain, base, b, 8)[:1]
        out_ref[:, b * 128 : (b + 1) * 128] = part + skip * value.astype(F32)


def local(pick, value, writers, readers, cum, cum_t, step_t, skip_gain):
    whole = lambda shape: pl.BlockSpec(shape, lambda i, p: (0, 0))
    mine = pl.BlockSpec((PER, TOK), lambda i, p: (p[0], 0))
    return pl.pallas_call(
        local_kernel,
        grid_spec=pltpu.PrefetchScalarGridSpec(
            num_scalar_prefetch=1,
            grid=(1,),
            in_specs=[whole((TOK, GCOLS)), whole((TOK, STATE)), whole((TOK, STATE)), whole((TOK, HEADS)),
                      mine, mine, whole((1, HEADS))],
            out_specs=whole((TOK, GCOLS)),
        ),
        out_shape=jax.ShapeDtypeStruct((TOK, GCOLS), F32),
        compiler_params=params(),
        cost_estimate=pl.CostEstimate(flops=10**9, bytes_accessed=8 * 10**6, transcendentals=0),
    )(pick, value, writers, readers, cum, cum_t, step_t, skip_gain.reshape(1, HEADS))


def decays_of(ref):
    terms = ref[ROWS:].astype(F32)
    return terms[:NB] + terms[NB : 2 * NB] + terms[2 * NB :]


def total_kernel(x_ref, *refs):
    pays, out_ref = refs[:NX], refs[NX]
    for mine in range(NX):

        @pl.when(x_ref[0] == mine)
        def _(mine=mine):
            order = [pays[(mine - source) % NX] for source in range(NX)]
            decays = [decays_of(ref) for ref in order]
            product = decays[0]
            for decay in decays[1:]:
                product = product * decay
            hi, mid, low = three(product)
            for b in range(NB):
                rows = slice(b * STATE, (b + 1) * STATE)
                total = order[0][rows].astype(F32)
                for source in range(1, NX):
                    total = decays[source][b : b + 1] * total + order[source][rows].astype(F32)
                total = total.astype(BF16)
                tail = jnp.concatenate(
                    [hi[b : b + 1], mid[b : b + 1], low[b : b + 1], jnp.zeros((5, 128), F32)], 0
                ).astype(BF16)
                for part in range(STATE // SROWS):
                    at = b * (STATE // SROWS) + part
                    out_ref[at, :SROWS] = total[part * SROWS : (part + 1) * SROWS]
                    out_ref[at, SROWS:] = tail


SMEM = pl.BlockSpec(memory_space=pltpu.SMEM)
VMEM = pl.BlockSpec(memory_space=pltpu.VMEM)


def row_total(x, pays):
    return pl.pallas_call(
        total_kernel,
        in_specs=[SMEM] + [VMEM] * NX,
        out_specs=VMEM,
        out_shape=jax.ShapeDtypeStruct((SHARES, TROWS, 128), BF16),
        compiler_params=params(),
    )(x, *pays)


def row_of(rows_ref, at):
    block = rows_ref[at].astype(F32)
    tail = block[SROWS:]
    return block[:SROWS], tail[:1] + tail[1:2] + tail[2:3]


def group_kernel(rows_ref, out_ref):
    for y in range(NY):
        total, product = row_of(rows_ref, y * NZ)
        for z in range(1, NZ):
            state, decay = row_of(rows_ref, y * NZ + z)
            total = decay * total + state
            product = decay * product
        out_ref[y, :SROWS] = total
        out_ref[y, SROWS:] = jnp.broadcast_to(product, (8, 128))


def group_total(rows):
    return pl.pallas_call(
        group_kernel,
        in_specs=[VMEM],
        out_specs=VMEM,
        out_shape=jax.ShapeDtypeStruct((NY, TROWS, 128), F32),
        compiler_params=params(),
    )(rows)


def scan_kernel(core_ref, rows_ref, own_ref, other_ref, out_ref):
    first = core_ref[0] == 0
    entry = jnp.zeros((SROWS, 128), F32)
    for y in range(NY):
        own, other = own_ref[y], other_ref[y]
        one = jnp.where(first, own, other)
        two = jnp.where(first, other, own)
        middle = one[SROWS : SROWS + 1] * entry + one[:SROWS]
        state = jnp.where(first, entry, middle)
        entry = two[SROWS : SROWS + 1] * middle + two[:SROWS]
        for z in range(NZ):
            out_ref[y * NZ + z] = state.astype(BF16)
            if z < NZ - 1:
                term, decay = row_of(rows_ref, y * NZ + z)
                state = decay * state + term


def scan(core, rows, own, other):
    return pl.pallas_call(
        scan_kernel,
        in_specs=[SMEM] + [VMEM] * 3,
        out_specs=VMEM,
        out_shape=jax.ShapeDtypeStruct((SHARES, SROWS, 128), BF16),
        compiler_params=params(),
    )(core, rows, own, other)


def enter_kernel(x_ref, entry_ref, *refs):
    pays, outs = refs[:NX], refs[NX:]
    for mine in range(NX):

        @pl.when(x_ref[0] == mine)
        def _(mine=mine):
            decays = [decays_of(pays[(mine - source) % NX]) for source in range(NX - 1)]
            for b in range(NB):
                rows = slice(b * STATE, (b + 1) * STATE)
                state = entry_ref[rows].astype(F32)
                for target in range(NX):
                    outs[(target - mine) % NX][rows] = state.astype(BF16)
                    if target < NX - 1:
                        term = pays[(mine - target) % NX][rows].astype(F32)
                        state = decays[target][b : b + 1] * state + term


def enter(x, entry, pays):
    return pl.pallas_call(
        enter_kernel,
        in_specs=[SMEM] + [VMEM] * (NX + 1),
        out_specs=[VMEM] * NX,
        out_shape=[jax.ShapeDtypeStruct((ROWS, 128), BF16)] * NX,
        compiler_params=params(),
    )(x, entry, *pays)


def final_kernel(pick_ref, rea_ref, state_ref, growth_ref, part_ref, *refs):
    out_ref = refs[-1]
    step = pl.program_id(0)
    base = pick_ref[0] * PER
    growth = growth_ref[...]
    for pair in range(CB // 2):
        at = 2 * pair * STATE
        both = jnp.concatenate([state_ref[at : at + STATE], state_ref[at + STATE : at + 2 * STATE]], 1)
        carried = jnp.dot(rea_ref[...], both, preferred_element_type=F32)
        for half in range(2):
            b = 2 * pair + half
            cols = slice(b * 128, (b + 1) * 128)
            grow = lanes_of(growth, base, step * CB + b, TOK)
            result = part_ref[:, cols] + carried[:, half * 128 : (half + 1) * 128] * grow
            out_ref[:, cols] = result.astype(BF16)


def final(pick, readers, state, growth, part, so_far):
    width = CB * 128
    whole = lambda shape: pl.BlockSpec(shape, lambda i, p: (0, 0))
    extra = [] if so_far is None else [so_far]
    return pl.pallas_call(
        final_kernel,
        grid_spec=pltpu.PrefetchScalarGridSpec(
            num_scalar_prefetch=1,
            grid=(CHUNKS,),
            in_specs=[
                whole((TOK, STATE)),
                pl.BlockSpec((CB * STATE, 128), lambda i, p: (i, 0)),
                whole((TOK, HEADS)),
                pl.BlockSpec((TOK, width), lambda i, p: (0, i)),
            ]
            + [pl.BlockSpec(memory_space=pl.ANY)] * len(extra),
            out_specs=pl.BlockSpec((TOK, width), lambda i, p: (0, p[0] * CHUNKS + i)),
        ),
        out_shape=jax.ShapeDtypeStruct((TOK, HCOLS), BF16),
        input_output_aliases={5: 0} if extra else {},
        compiler_params=params(),
        cost_estimate=pl.CostEstimate(flops=10**8, bytes_accessed=2 * 10**6, transcendentals=0),
    )(pick, readers, state, growth, part, *extra)


def turned(value, steps):
    return lax.ppermute(value, "x", [(i, (i + steps) % NX) for i in range(NX)])


def body(conv_input, conv_weight, step_raw, decay_log, skip_gain):
    count = lax.axis_size(AXES)
    edge = lax.ppermute(conv_input[TOK - KERNEL + 1 :], AXES, [(i, i + 1) for i in range(count - 1)])
    x = lax.axis_index("x").reshape(1)
    core = lax.axis_index("core").reshape(1)
    picks = [(x + ahead) % NX for ahead in range(NX)]
    cum, factor, growth, cum_t, step_t, decay = prep(step_raw, decay_log)
    made, pays = {}, {}
    for ahead in (1, 3, 2, 0):
        made[ahead] = states(picks[ahead], conv_input, edge, conv_weight, factor, decay)
        pays[ahead] = turned(made[ahead][0], ahead) if ahead else made[ahead][0]
    pays = [pays[d] for d in range(NX)]
    parts = [
        local(picks[d], *made[d][1:], cum, cum_t, step_t, skip_gain) for d in range(NX)
    ]
    rows = lax.all_to_all(row_total(x, pays), ("y", "z"), 0, 0, tiled=True)
    own = group_total(rows)
    other = lax.ppermute(own, "core", [(0, 1), (1, 0)])
    entry = lax.all_to_all(scan(core, rows, own, other), ("y", "z"), 0, 0, tiled=True)
    entering = enter(x, entry.reshape(ROWS, 128), pays)
    out = None
    for ahead in (0, 1, 3, 2):
        state = turned(entering[ahead], ahead) if ahead else entering[0]
        d = (NX - ahead) % NX
        out = final(picks[d], made[d][3], state, growth, parts[d], out)
    return out


def solution(mesh):
    fine = Mesh(mesh.devices.reshape(NY, 2, NZ, NX), AXES)
    in_specs = (P(AXES, None), P(), P(AXES, None), P(), P())
    return jax.shard_map(body, mesh=fine, in_specs=in_specs, out_specs=P(AXES, None), check_vma=False)
```

```python
import functools

import jax
import jax.numpy as jnp
from jax import lax
from jax.experimental import pallas as pl
from jax.experimental.pallas import tpu as pltpu
from jax.sharding import Mesh, PartitionSpec as P

HEADS = 128
HEAD_DIM = 64
STATE = 128
GROUPS = 4
KERNEL = 4
TOK = 128
PER = HEADS // GROUPS
GCOLS = PER * HEAD_DIM
NB = GCOLS // 128
HCOLS = HEADS * HEAD_DIM
ROWS = NB * STATE
PAY = ROWS + 3 * NB
SHARES = 64
SROWS = ROWS // SHARES
TROWS = SROWS + 8
NX, NY, NZ = 4, 8, 8
F32 = jnp.float32
BF16 = jnp.bfloat16
LIMIT = 12 * 1024 * 1024
PREP_LIMIT = 12 * 1024 * 1024
AXES = ("y", "core", "z", "x")
SMEM = pl.BlockSpec(memory_space=pltpu.SMEM)
VMEM = pl.BlockSpec(memory_space=pltpu.VMEM)
HBM = pl.BlockSpec(memory_space=pltpu.HBM)
ANY = pl.BlockSpec(memory_space=pl.ANY)


def params(limit=LIMIT):
    return pltpu.CompilerParams(vmem_limit_bytes=limit)


def three(v):
    hi = v.astype(BF16).astype(F32)
    mid = (v - hi).astype(BF16).astype(F32)
    low = (v - hi - mid).astype(BF16).astype(F32)
    return hi, mid, low


def lanes_of(per_head, base, block, rows):
    lane = lax.broadcasted_iota(jnp.int32, (rows, 128), 1)
    pick = base + 2 * block + lane // HEAD_DIM
    return jnp.take_along_axis(per_head, pick, axis=1)


def prep_kernel(
    x_hbm, raw_hbm, log_hbm,
    x_ref, edge_ref, cum_ref, factor_ref, growth_ref, cum_t_ref, step_t_ref, decay_ref,
    raw_ref, log_ref, sems,
):
    raw_copy = pltpu.make_async_copy(raw_hbm, raw_ref, sems.at[0])
    log_copy = pltpu.make_async_copy(log_hbm, log_ref, sems.at[1])
    copy = pltpu.make_async_copy(x_hbm, x_ref, sems.at[2])
    raw_copy.start()
    log_copy.start()
    copy.start()
    raw_copy.wait()
    log_copy.wait()
    raw = raw_ref[...]
    step = jnp.maximum(raw, 0.0) + jnp.log1p(jnp.exp(-jnp.abs(raw)))
    cum = -jnp.exp(log_ref[...]) * step
    row = lax.broadcasted_iota(jnp.int32, (TOK, HEADS), 0)
    shift = 1
    while shift < TOK:
        cum = cum + jnp.where(row >= shift, pltpu.roll(cum, shift, 0), 0.0)
        shift *= 2
    last = cum[TOK - 1 :, :]
    cum_ref[...] = cum
    factor_ref[...] = jnp.exp(last - cum) * step
    growth_ref[...] = jnp.exp(cum)
    cum_t_ref[...] = cum.T
    step_t_ref[...] = step.T
    decay_ref[...] = jnp.broadcast_to(jnp.exp(last), (8, HEADS))
    copy.wait()
    edge_ref[...] = x_ref[TOK - 16 :, :].astype(F32)[16 - KERNEL + 1 :].astype(BF16)


def prep(conv_input, step_raw, decay_log):
    square = jax.ShapeDtypeStruct((TOK, HEADS), F32)
    channels = conv_input.shape[1]
    return pl.pallas_call(
        prep_kernel,
        in_specs=[HBM] * 3,
        out_specs=[VMEM] * 8,
        out_shape=[
            jax.ShapeDtypeStruct((TOK, channels), BF16),
            jax.ShapeDtypeStruct((KERNEL - 1, channels), BF16),
            *[square] * 5,
            jax.ShapeDtypeStruct((8, HEADS), F32),
        ],
        scratch_shapes=[
            pltpu.VMEM((TOK, HEADS), F32), pltpu.VMEM((1, HEADS), F32), pltpu.SemaphoreType.DMA((3,))
        ],
        compiler_params=params(PREP_LIMIT),
    )(conv_input, step_raw, decay_log.reshape(1, HEADS))


def convolve(x_ref, edge_ref, w_ref, at):
    cols = pl.ds(pl.multiple_of(at, 128), 128)
    x = x_ref[:, cols].astype(F32)
    edge = edge_ref[:, cols].astype(F32)
    weight = w_ref[:, cols]
    wide = jnp.concatenate([jnp.zeros((8 - KERNEL + 1, 128), F32), edge, x], 0)
    out = None
    for tap in range(KERNEL):
        first = 8 - KERNEL + 1 + tap
        term = wide[first : first + TOK] * weight[tap : tap + 1]
        out = term if out is None else out + term
    return out.astype(BF16)


def group_of(x_ref, ahead):
    return jnp.bitwise_and(x_ref[0] + ahead, NX - 1)


def state_kernel(
    ahead, x_ref, in_ref, edge_ref, w_ref, factor_ref, decay_ref, pay_ref, val_ref, wri_ref, rea_ref
):
    group = group_of(x_ref, ahead)
    base = group * PER
    writers = convolve(in_ref, edge_ref, w_ref, HCOLS + group * STATE)
    wri_ref[...] = writers
    turned_writers = writers.astype(F32).T.astype(BF16)
    rows = [lanes_of(decay_ref[...], base, b, 8)[:1] for b in range(NB)]
    for at, term in enumerate(three(jnp.concatenate(rows, 0))):
        pay_ref[ROWS + at * NB : ROWS + (at + 1) * NB] = term.astype(BF16)
    factor = factor_ref[...]
    for pair in range(NB // 2):
        weighted = []
        for b in (2 * pair, 2 * pair + 1):
            value = convolve(in_ref, edge_ref, w_ref, group * GCOLS + b * 128)
            val_ref[:, b * 128 : (b + 1) * 128] = value
            fac = lanes_of(factor, base, b, TOK)
            weighted.append((value.astype(F32) * fac).astype(BF16))
        state = jnp.dot(turned_writers, jnp.concatenate(weighted, 1), preferred_element_type=F32)
        for half in range(2):
            b = 2 * pair + half
            pay_ref[b * STATE : (b + 1) * STATE] = state[:, half * 128 : (half + 1) * 128].astype(BF16)
    rea_ref[...] = convolve(in_ref, edge_ref, w_ref, HCOLS + (GROUPS + group) * STATE)


def states(ahead, x, conv_input, edge, conv_weight, factor, decay):
    return pl.pallas_call(
        functools.partial(state_kernel, ahead),
        in_specs=[SMEM] + [VMEM] * 5,
        out_specs=[VMEM] * 4,
        out_shape=[
            jax.ShapeDtypeStruct((PAY, 128), BF16),
            jax.ShapeDtypeStruct((TOK, GCOLS), BF16),
            jax.ShapeDtypeStruct((TOK, STATE), BF16),
            jax.ShapeDtypeStruct((TOK, STATE), BF16),
        ],
        compiler_params=params(),
        cost_estimate=pl.CostEstimate(flops=10**8, bytes_accessed=3 * 10**6, transcendentals=0),
    )(x, conv_input, edge, conv_weight, factor, decay)


def local_kernel(
    ahead, x_ref, val_ref, wri_ref, rea_ref, cum_ref, cum_t_ref, step_t_ref, gain_ref, out_ref
):
    base = group_of(x_ref, ahead) * PER
    mine = pl.ds(pl.multiple_of(base, PER), PER)
    cum_t = cum_t_ref[mine]
    step_t = step_t_ref[mine]
    affinity = lax.dot_general(
        rea_ref[...], wri_ref[...], (((1,), (1,)), ((), ())), preferred_element_type=F32
    )
    cum = cum_ref[...]
    gain = jnp.broadcast_to(gain_ref[...], (8, HEADS))
    row = lax.broadcasted_iota(jnp.int32, (TOK, TOK), 0)
    col = lax.broadcasted_iota(jnp.int32, (TOK, TOK), 1)
    causal = row >= col
    first = col < HEAD_DIM
    for b in range(NB):
        scores = []
        for half in range(2):
            h = 2 * b + half
            at = jnp.take_along_axis(cum, jnp.full((TOK, TOK), base + h, jnp.int32), axis=1)
            span = jnp.where(causal, at - cum_t[h : h + 1], -1e30)
            weight = jnp.exp(span) * step_t[h : h + 1]
            scores.append((weight * affinity).astype(BF16))
        value = val_ref[:, b * 128 : (b + 1) * 128]
        zero = jnp.zeros_like(value)
        apart = jnp.concatenate([jnp.where(first, value, zero), jnp.where(first, zero, value)], 0)
        part = jnp.dot(jnp.concatenate(scores, 1), apart, preferred_element_type=F32)
        skip = lanes_of(gain, base, b, 8)[:1]
        out_ref[:, b * 128 : (b + 1) * 128] = part + skip * value.astype(F32)


def local(ahead, x, value, writers, readers, cum, cum_t, step_t, skip_gain):
    return pl.pallas_call(
        functools.partial(local_kernel, ahead),
        in_specs=[SMEM] + [VMEM] * 7,
        out_specs=VMEM,
        out_shape=jax.ShapeDtypeStruct((TOK, GCOLS), F32),
        compiler_params=params(),
        cost_estimate=pl.CostEstimate(flops=10**9, bytes_accessed=8 * 10**6, transcendentals=0),
    )(x, value, writers, readers, cum, cum_t, step_t, skip_gain.reshape(1, HEADS))


def decays_of(ref):
    terms = ref[ROWS:].astype(F32)
    return terms[:NB] + terms[NB : 2 * NB] + terms[2 * NB :]


def total_kernel(x_ref, *refs):
    pays, out_ref = refs[:NX], refs[NX]
    for mine in range(NX):

        @pl.when(x_ref[0] == mine)
        def _(mine=mine):
            order = [pays[(mine - source) % NX] for source in range(NX)]
            decays = [decays_of(ref) for ref in order]
            product = decays[0]
            for decay in decays[1:]:
                product = product * decay
            hi, mid, low = three(product)
            for b in range(NB):
                rows = slice(b * STATE, (b + 1) * STATE)
                total = order[0][rows].astype(F32)
                for source in range(1, NX):
                    total = decays[source][b : b + 1] * total + order[source][rows].astype(F32)
                total = total.astype(BF16)
                tail = jnp.concatenate(
                    [hi[b : b + 1], mid[b : b + 1], low[b : b + 1], jnp.zeros((5, 128), F32)], 0
                ).astype(BF16)
                for part in range(STATE // SROWS):
                    at = b * (STATE // SROWS) + part
                    out_ref[at, :SROWS] = total[part * SROWS : (part + 1) * SROWS]
                    out_ref[at, SROWS:] = tail


def row_total(x, pays):
    return pl.pallas_call(
        total_kernel,
        in_specs=[SMEM] + [VMEM] * NX,
        out_specs=VMEM,
        out_shape=jax.ShapeDtypeStruct((SHARES, TROWS, 128), BF16),
        compiler_params=params(),
    )(x, *pays)


def row_of(rows_ref, at):
    block = rows_ref[at].astype(F32)
    tail = block[SROWS:]
    return block[:SROWS], tail[:1] + tail[1:2] + tail[2:3]


def group_kernel(rows_ref, out_ref):
    for y in range(NY):
        total, product = row_of(rows_ref, y * NZ)
        for z in range(1, NZ):
            state, decay = row_of(rows_ref, y * NZ + z)
            total = decay * total + state
            product = decay * product
        out_ref[y, :SROWS] = total
        out_ref[y, SROWS:] = jnp.broadcast_to(product, (8, 128))


def group_total(rows):
    return pl.pallas_call(
        group_kernel,
        in_specs=[VMEM],
        out_specs=VMEM,
        out_shape=jax.ShapeDtypeStruct((NY, TROWS, 128), F32),
        compiler_params=params(),
    )(rows)


def scan_kernel(core_ref, rows_ref, own_ref, other_ref, out_ref):
    first = core_ref[0] == 0
    entry = jnp.zeros((SROWS, 128), F32)
    for y in range(NY):
        own, other = own_ref[y], other_ref[y]
        one = jnp.where(first, own, other)
        two = jnp.where(first, other, own)
        middle = one[SROWS : SROWS + 1] * entry + one[:SROWS]
        state = jnp.where(first, entry, middle)
        entry = two[SROWS : SROWS + 1] * middle + two[:SROWS]
        for z in range(NZ):
            out_ref[y * NZ + z] = state.astype(BF16)
            if z < NZ - 1:
                term, decay = row_of(rows_ref, y * NZ + z)
                state = decay * state + term


def scan(core, rows, own, other):
    return pl.pallas_call(
        scan_kernel,
        in_specs=[SMEM] + [VMEM] * 3,
        out_specs=VMEM,
        out_shape=jax.ShapeDtypeStruct((SHARES, SROWS, 128), BF16),
        compiler_params=params(),
    )(core, rows, own, other)


def enter_kernel(x_ref, entry_ref, *refs):
    pays, outs = refs[:NX], refs[NX:]
    for mine in range(NX):

        @pl.when(x_ref[0] == mine)
        def _(mine=mine):
            decays = [decays_of(pays[(mine - source) % NX]) for source in range(NX - 1)]
            for b in range(NB):
                rows = slice(b * STATE, (b + 1) * STATE)
                state = entry_ref[rows].astype(F32)
                for target in range(NX):
                    outs[(target - mine) % NX][rows] = state.astype(BF16)
                    if target < NX - 1:
                        term = pays[(mine - target) % NX][rows].astype(F32)
                        state = decays[target][b : b + 1] * state + term


def enter(x, entry, pays):
    return pl.pallas_call(
        enter_kernel,
        in_specs=[SMEM] + [VMEM] * (NX + 1),
        out_specs=[VMEM] * NX,
        out_shape=[jax.ShapeDtypeStruct((ROWS, 128), BF16)] * NX,
        compiler_params=params(),
    )(x, entry, *pays)


PIECES = 4


def final_kernel(ahead, x_ref, rea_ref, state_ref, growth_ref, part_ref, *refs):
    out_ref, buf, sems = refs[-3:]
    group = group_of(x_ref, ahead)
    growth = growth_ref[...]
    readers = rea_ref[...]
    copies = []
    for pair in range(NB // 2):
        at = 2 * pair * STATE
        both = jnp.concatenate([state_ref[at : at + STATE], state_ref[at + STATE : at + 2 * STATE]], 1)
        carried = jnp.dot(readers, both, preferred_element_type=F32)
        for half in range(2):
            b = 2 * pair + half
            cols = slice(b * 128, (b + 1) * 128)
            grow = lanes_of(growth, group * PER, b, TOK)
            result = part_ref[:, cols] + carried[:, half * 128 : (half + 1) * 128] * grow
            buf[:, cols] = result.astype(BF16)
        if (pair + 1) % (NB // 2 // PIECES) == 0:
            piece = len(copies)
            width = GCOLS // PIECES
            to = pl.multiple_of(group * GCOLS + piece * width, width)
            copies.append(
                pltpu.make_async_copy(
                    buf.at[:, pl.ds(piece * width, width)], out_ref.at[:, pl.ds(to, width)], sems.at[piece]
                )
            )
            copies[-1].start()
    for copy in copies:
        copy.wait()


def final(ahead, x, readers, state, growth, part, so_far):
    extra = [] if so_far is None else [so_far]
    return pl.pallas_call(
        functools.partial(final_kernel, ahead),
        in_specs=[SMEM] + [VMEM] * 4 + [ANY] * len(extra),
        out_specs=ANY,
        out_shape=jax.ShapeDtypeStruct((TOK, HCOLS), BF16),
        scratch_shapes=[pltpu.VMEM((TOK, GCOLS), BF16), pltpu.SemaphoreType.DMA((PIECES,))],
        input_output_aliases={5: 0} if extra else {},
        compiler_params=params(),
        cost_estimate=pl.CostEstimate(flops=10**8, bytes_accessed=2 * 10**6, transcendentals=0),
    )(x, readers, state, growth, part, *extra)


def turned(value, steps):
    return lax.ppermute(value, "x", [(i, (i + steps) % NX) for i in range(NX)])


def body(conv_input, conv_weight, step_raw, decay_log, skip_gain):
    count = lax.axis_size(AXES)
    x = lax.axis_index("x").reshape(1)
    core = lax.axis_index("core").reshape(1)
    held, edge, cum, factor, growth, cum_t, step_t, decay = prep(conv_input, step_raw, decay_log)
    edge = lax.ppermute(edge, AXES, [(i, i + 1) for i in range(count - 1)])
    made, pays = {}, {}
    for ahead in (2, 1, 3, 0):
        made[ahead] = states(ahead, x, held, edge, conv_weight, factor, decay)
        pays[ahead] = turned(made[ahead][0], ahead) if ahead else made[ahead][0]
    parts = {d: local(d, x, *made[d][1:], cum, cum_t, step_t, skip_gain) for d in (2, 1, 3, 0)}
    pays, parts = lax.optimization_barrier((pays, parts))
    pays = [pays[d] for d in range(NX)]
    rows = lax.all_to_all(row_total(x, pays), ("y", "z"), 0, 0, tiled=True)
    own = group_total(rows)
    other = lax.ppermute(own, "core", [(0, 1), (1, 0)])
    entry = lax.all_to_all(scan(core, rows, own, other), ("y", "z"), 0, 0, tiled=True)
    entering = enter(x, entry.reshape(ROWS, 128), pays)
    out = None
    for ahead in (0, 2, 1, 3):
        state = turned(entering[ahead], ahead) if ahead else entering[0]
        d = (NX - ahead) % NX
        out = final(d, x, made[d][3], state, growth, parts[d], out)
    return out


def solution(mesh):
    fine = Mesh(mesh.devices.reshape(NY, 2, NZ, NX), AXES)
    in_specs = (P(AXES, None), P(), P(AXES, None), P(), P())
    return jax.shard_map(body, mesh=fine, in_specs=in_specs, out_specs=P(AXES, None), check_vma=False)
```

```python
import functools

import jax
import jax.numpy as jnp
from jax import lax
from jax.experimental import pallas as pl
from jax.experimental.pallas import tpu as pltpu
from jax.sharding import Mesh, PartitionSpec as P

HEADS = 128
HEAD_DIM = 64
STATE = 128
GROUPS = 4
KERNEL = 4
TOK = 128
PER = HEADS // GROUPS
GCOLS = PER * HEAD_DIM
NB = GCOLS // 128
HCOLS = HEADS * HEAD_DIM
PARTS = 1
NBP = NB // PARTS
PCOLS = NBP * 128
ROWS = NBP * STATE
TAIL = max(32, 3 * NBP)
PAY = ROWS + TAIL
SHARES = 64
SROWS = ROWS // SHARES
TROWS = SROWS + 8
NX, NY, NZ = 4, 8, 8
F32 = jnp.float32
BF16 = jnp.bfloat16
LIMIT = 12 * 1024 * 1024
AXES = ("y", "core", "z", "x")
SENT = (2, 1, 3, 0)
SMEM = pl.BlockSpec(memory_space=pltpu.SMEM)
VMEM = pl.BlockSpec(memory_space=pltpu.VMEM)
ANY = pl.BlockSpec(memory_space=pl.ANY)


def params():
    return pltpu.CompilerParams(vmem_limit_bytes=LIMIT)


def three(v):
    hi = v.astype(BF16).astype(F32)
    mid = (v - hi).astype(BF16).astype(F32)
    low = (v - hi - mid).astype(BF16).astype(F32)
    return hi, mid, low


def lanes_of(per_head, base, block, rows):
    lane = lax.broadcasted_iota(jnp.int32, (rows, 128), 1)
    pick = base + 2 * block + lane // HEAD_DIM
    return jnp.take_along_axis(per_head, pick, axis=1)


def prep_kernel(x_hbm, raw_ref, log_ref, x_ref, early_ref, late_ref, sem):
    copy = pltpu.make_async_copy(x_hbm, x_ref, sem)
    copy.start()
    raw = raw_ref[...]
    step = jnp.maximum(raw, 0.0) + jnp.log1p(jnp.exp(-jnp.abs(raw)))
    cum = -jnp.exp(log_ref[...]) * step
    row = lax.broadcasted_iota(jnp.int32, (TOK, HEADS), 0)
    shift = 1
    while shift < TOK:
        cum = cum + jnp.where(row >= shift, pltpu.roll(cum, shift, 0), 0.0)
        shift *= 2
    last = cum[TOK - 1 :, :]
    early_ref[:TOK] = jnp.exp(last - cum) * step
    early_ref[TOK:] = jnp.broadcast_to(jnp.exp(last), (8, HEADS))
    late_ref[:TOK] = cum
    late_ref[TOK : 2 * TOK] = cum.T
    late_ref[2 * TOK :] = step.T
    copy.wait()


def prep(conv_input, step_raw, decay_log):
    channels = conv_input.shape[1]
    return pl.pallas_call(
        prep_kernel,
        in_specs=[ANY, VMEM, VMEM],
        out_specs=[VMEM] * 3,
        out_shape=[
            jax.ShapeDtypeStruct((TOK, channels), BF16),
            jax.ShapeDtypeStruct((TOK + 8, HEADS), F32),
            jax.ShapeDtypeStruct((2 * TOK + HEADS, HEADS), F32),
        ],
        scratch_shapes=[pltpu.SemaphoreType.DMA],
        compiler_params=params(),
        cost_estimate=pl.CostEstimate(flops=0, bytes_accessed=0, transcendentals=0),
    )(conv_input, step_raw, decay_log.reshape(1, HEADS))


def convolve(x_ref, edge_ref, w_ref, at):
    cols = pl.ds(pl.multiple_of(at, 128), 128)
    x = x_ref[:, cols].astype(F32)
    edge = edge_ref[:, cols].astype(F32)
    weight = w_ref[:, cols]
    wide = jnp.concatenate([jnp.zeros((8 - KERNEL + 1, 128), F32), edge, x], 0)
    out = None
    for tap in range(KERNEL):
        first = 8 - KERNEL + 1 + tap
        term = wide[first : first + TOK] * weight[tap : tap + 1]
        out = term if out is None else out + term
    return out.astype(BF16)


def group_of(x_ref, ahead):
    return jnp.bitwise_and(x_ref[0] + ahead, NX - 1)


def state_kernel(ahead, part, x_ref, in_ref, edge_ref, w_ref, early_ref, pay_ref):
    group = group_of(x_ref, ahead)
    base = group * PER + part * 2 * NBP
    writers = convolve(in_ref, edge_ref, w_ref, HCOLS + group * STATE).astype(F32).T.astype(BF16)
    decay = early_ref[TOK:]
    rows = [lanes_of(decay, base, b, 8)[:1] for b in range(NBP)]
    terms = three(jnp.concatenate(rows, 0))
    if TAIL > 3 * NBP:
        terms += (jnp.zeros((TAIL - 3 * NBP, 128), F32),)
    pay_ref[ROWS:] = jnp.concatenate(terms, 0).astype(BF16)
    factor = early_ref[:TOK]
    for pair in range(NBP // 2):
        weighted = []
        for b in (2 * pair, 2 * pair + 1):
            value = convolve(in_ref, edge_ref, w_ref, group * GCOLS + part * PCOLS + b * 128)
            fac = lanes_of(factor, base, b, TOK)
            weighted.append((value.astype(F32) * fac).astype(BF16))
        state = jnp.dot(writers, jnp.concatenate(weighted, 1), preferred_element_type=F32)
        for half in range(2):
            b = 2 * pair + half
            pay_ref[b * STATE : (b + 1) * STATE] = state[:, half * 128 : (half + 1) * 128].astype(BF16)


def states(ahead, part, *args):
    return pl.pallas_call(
        functools.partial(state_kernel, ahead, part),
        in_specs=[SMEM] + [VMEM] * 4,
        out_specs=VMEM,
        out_shape=jax.ShapeDtypeStruct((PAY, 128), BF16),
        compiler_params=params(),
        cost_estimate=pl.CostEstimate(flops=10**8, bytes_accessed=3 * 10**6, transcendentals=0),
    )(*args)


def decays_of(ref):
    terms = ref[ROWS:].astype(F32)
    return terms[:NBP] + terms[NBP : 2 * NBP] + terms[2 * NBP : 3 * NBP]


def total_kernel(x_ref, *refs):
    pays, out_ref = refs[:NX], refs[NX]
    for mine in range(NX):

        @pl.when(x_ref[0] == mine)
        def _(mine=mine):
            order = [pays[SENT.index((mine - source) % NX)] for source in range(NX)]
            decays = [decays_of(ref) for ref in order]
            product = decays[0]
            for decay in decays[1:]:
                product = product * decay
            hi, mid, low = three(product)
            for b in range(NBP):
                rows = slice(b * STATE, (b + 1) * STATE)
                total = order[0][rows].astype(F32)
                for source in range(1, NX):
                    total = decays[source][b : b + 1] * total + order[source][rows].astype(F32)
                tail = jnp.concatenate(
                    [hi[b : b + 1], mid[b : b + 1], low[b : b + 1], jnp.zeros((5, 128), F32)], 0
                )
                for part in range(STATE // SROWS):
                    share = jnp.concatenate([total[part * SROWS : (part + 1) * SROWS], tail], 0)
                    out_ref[b * (STATE // SROWS) + part] = share.astype(BF16)


def row_total(x, pays):
    return pl.pallas_call(
        total_kernel,
        in_specs=[SMEM] + [VMEM] * NX,
        out_specs=VMEM,
        out_shape=jax.ShapeDtypeStruct((SHARES, TROWS, 128), BF16),
        compiler_params=params(),
    )(x, *pays)


def row_of(rows_ref, at):
    block = rows_ref[at].astype(F32)
    tail = block[SROWS:]
    return block[:SROWS], tail[:1] + tail[1:2] + tail[2:3]


def group_kernel(rows_ref, out_ref):
    for y in range(NY):
        total, product = row_of(rows_ref, y * NZ)
        for z in range(1, NZ):
            state, decay = row_of(rows_ref, y * NZ + z)
            total = decay * total + state
            product = decay * product
        out_ref[y, :SROWS] = total
        out_ref[y, SROWS:] = jnp.broadcast_to(product, (8, 128))


def group_total(rows):
    return pl.pallas_call(
        group_kernel,
        in_specs=[VMEM],
        out_specs=VMEM,
        out_shape=jax.ShapeDtypeStruct((NY, TROWS, 128), F32),
        compiler_params=params(),
    )(rows)


def scan_kernel(core_ref, rows_ref, own_ref, other_ref, out_ref):
    first = core_ref[0] == 0
    entry = jnp.zeros((SROWS, 128), F32)
    for y in range(NY):
        own, other = own_ref[y], other_ref[y]
        one = jnp.where(first, own, other)
        two = jnp.where(first, other, own)
        middle = one[SROWS : SROWS + 1] * entry + one[:SROWS]
        state = jnp.where(first, entry, middle)
        entry = two[SROWS : SROWS + 1] * middle + two[:SROWS]
        for z in range(NZ):
            out_ref[y * NZ + z] = state.astype(BF16)
            if z < NZ - 1:
                term, decay = row_of(rows_ref, y * NZ + z)
                state = decay * state + term


def scan(core, rows, own, other):
    return pl.pallas_call(
        scan_kernel,
        in_specs=[SMEM] + [VMEM] * 3,
        out_specs=VMEM,
        out_shape=jax.ShapeDtypeStruct((SHARES, SROWS, 128), BF16),
        compiler_params=params(),
    )(core, rows, own, other)


def enter_kernel(x_ref, entry_ref, *refs):
    pays, outs = refs[:NX], refs[NX:]
    for mine in range(NX):

        @pl.when(x_ref[0] == mine)
        def _(mine=mine):
            decays = [decays_of(pays[SENT.index((mine - source) % NX)]) for source in range(NX - 1)]
            for b in range(NBP):
                rows = slice(b * STATE, (b + 1) * STATE)
                state = entry_ref[rows].astype(F32)
                for target in range(NX):
                    outs[(target - mine) % NX][rows] = state.astype(BF16)
                    if target < NX - 1:
                        term = pays[SENT.index((mine - target) % NX)][rows].astype(F32)
                        state = decays[target][b : b + 1] * state + term


def enter(x, entry, pays):
    return pl.pallas_call(
        enter_kernel,
        in_specs=[SMEM] + [VMEM] * (NX + 1),
        out_specs=[VMEM] * NX,
        out_shape=[jax.ShapeDtypeStruct((ROWS, 128), BF16)] * NX,
        compiler_params=params(),
    )(x, entry, *pays)


def local_kernel(ahead, x_ref, in_ref, edge_ref, w_ref, late_ref, gain_ref, out_ref, rea_ref):
    group = group_of(x_ref, ahead)
    base = group * PER
    writers = convolve(in_ref, edge_ref, w_ref, HCOLS + group * STATE)
    readers = convolve(in_ref, edge_ref, w_ref, HCOLS + (GROUPS + group) * STATE)
    rea_ref[...] = readers
    affinity = lax.dot_general(
        readers, writers, (((1,), (1,)), ((), ())), preferred_element_type=F32
    )
    cum = late_ref[:TOK]
    cum_t = late_ref[pl.ds(pl.multiple_of(TOK + base, PER), PER)]
    step_t = late_ref[pl.ds(pl.multiple_of(TOK + HEADS + base, PER), PER)]
    gain = jnp.broadcast_to(gain_ref[...], (8, HEADS))
    row = lax.broadcasted_iota(jnp.int32, (TOK, TOK), 0)
    col = lax.broadcasted_iota(jnp.int32, (TOK, TOK), 1)
    causal = row >= col
    first = col < HEAD_DIM
    for b in range(NB):
        scores = []
        for h in (2 * b, 2 * b + 1):
            here = jnp.take_along_axis(cum, jnp.full((TOK, TOK), base + h, jnp.int32), axis=1)
            span = jnp.where(causal, here - cum_t[h : h + 1], -1e30)
            weight = jnp.exp(span) * step_t[h : h + 1]
            scores.append((weight * affinity).astype(BF16))
        value = convolve(in_ref, edge_ref, w_ref, group * GCOLS + b * 128)
        zero = jnp.zeros_like(value)
        apart = jnp.concatenate([jnp.where(first, value, zero), jnp.where(first, zero, value)], 0)
        local = jnp.dot(jnp.concatenate(scores, 1), apart, preferred_element_type=F32)
        skip = lanes_of(gain, base, b, 8)[:1]
        out_ref[:, b * 128 : (b + 1) * 128] = local + skip * value.astype(F32)


def local(ahead, *args):
    return pl.pallas_call(
        functools.partial(local_kernel, ahead),
        in_specs=[SMEM] + [VMEM] * 5,
        out_specs=[VMEM] * 2,
        out_shape=[
            jax.ShapeDtypeStruct((TOK, GCOLS), F32),
            jax.ShapeDtypeStruct((TOK, STATE), BF16),
        ],
        compiler_params=params(),
        cost_estimate=pl.CostEstimate(flops=10**9, bytes_accessed=8 * 10**6, transcendentals=0),
    )(*args)


PIECES = 4


def final_kernel(ahead, x_ref, rea_ref, late_ref, part_ref, state_ref, *refs):
    out_ref, buf, sems = refs[-3:]
    group = group_of(x_ref, ahead)
    base = group * PER
    growth = jnp.exp(late_ref[:TOK])
    readers = rea_ref[...]
    width = GCOLS // PIECES
    copies = []
    for pair in range(NB // 2):
        at = 2 * pair * STATE
        both = jnp.concatenate([state_ref[at : at + STATE], state_ref[at + STATE : at + 2 * STATE]], 1)
        carried = jnp.dot(readers, both, preferred_element_type=F32)
        for half in range(2):
            b = 2 * pair + half
            cols = slice(b * 128, (b + 1) * 128)
            grow = lanes_of(growth, base, b, TOK)
            result = part_ref[:, cols] + carried[:, half * 128 : (half + 1) * 128] * grow
            buf[:, cols] = result.astype(BF16)
        if (pair + 1) % (NB // 2 // PIECES) == 0:
            piece = len(copies)
            to = pl.multiple_of(group * GCOLS + piece * width, width)
            copies.append(
                pltpu.make_async_copy(
                    buf.at[:, pl.ds(piece * width, width)], out_ref.at[:, pl.ds(to, width)], sems.at[piece]
                )
            )
            copies[-1].start()
    for copy in copies:
        copy.wait()


def final(ahead, so_far, *args):
    extra = [] if so_far is None else [so_far]
    return pl.pallas_call(
        functools.partial(final_kernel, ahead),
        in_specs=[SMEM] + [VMEM] * 4 + [ANY] * len(extra),
        out_specs=ANY,
        out_shape=jax.ShapeDtypeStruct((TOK, HCOLS), BF16),
        scratch_shapes=[pltpu.VMEM((TOK, GCOLS), BF16), pltpu.SemaphoreType.DMA((PIECES,))],
        input_output_aliases={5: 0} if extra else {},
        compiler_params=params(),
        cost_estimate=pl.CostEstimate(flops=10**8, bytes_accessed=2 * 10**6, transcendentals=0),
    )(*args, *extra)


def turned(value, steps):
    return lax.ppermute(value, "x", [(i, (i + steps) % NX) for i in range(NX)])


def body(conv_input, conv_weight, step_raw, decay_log, skip_gain):
    count = lax.axis_size(AXES)
    x = lax.axis_index("x").reshape(1)
    core = lax.axis_index("core").reshape(1)
    edge = lax.ppermute(conv_input[TOK - KERNEL + 1 :], AXES, [(i, i + 1) for i in range(count - 1)])
    held, early, late = prep(conv_input, step_raw, decay_log)
    pays = {}
    for ahead in SENT:
        state = states(ahead, 0, x, held, edge, conv_weight, early)
        pays[ahead] = turned(state, ahead) if ahead else state
    pays = [pays[d] for d in SENT]
    rows = lax.all_to_all(row_total(x, pays), ("y", "z"), 0, 0, tiled=True)
    own = group_total(rows)
    other = lax.ppermute(own, "core", [(0, 1), (1, 0)])
    entry = lax.all_to_all(scan(core, rows, own, other), ("y", "z"), 0, 0, tiled=True)
    entering = enter(x, entry.reshape(ROWS, 128), pays)
    late, entering = lax.optimization_barrier((late, entering))
    gain = skip_gain.reshape(1, HEADS)
    out = None
    for ahead in (0, 2, 1, 3):
        state = turned(entering[ahead], ahead) if ahead else entering[0]
        d = (NX - ahead) % NX
        part, readers = local(d, x, conv_input, edge, conv_weight, late, gain)
        out = final(d, out, x, readers, late, part, state)
    return out


def solution(mesh):
    fine = Mesh(mesh.devices.reshape(NY, 2, NZ, NX), AXES)
    in_specs = (P(AXES, None), P(), P(AXES, None), P(), P())
    return jax.shard_map(body, mesh=fine, in_specs=in_specs, out_specs=P(AXES, None), check_vma=False)
```

```python
import jax
import jax.numpy as jnp
from jax import lax
from jax.experimental import pallas as pl
from jax.experimental.pallas import tpu as pltpu
from jax.sharding import Mesh, PartitionSpec as P

HEADS = 128
HEAD_DIM = 64
STATE = 128
GROUPS = 4
KERNEL = 4
TOK = 128
PER = HEADS // GROUPS
NB = PER // 2
HCOLS = HEADS * HEAD_DIM
NX, NY, NZ = 4, 8, 8
NZL = 2
NZH = NZ // NZL
NEAR = NZL * NX
OWN = HEADS // NEAR
NBO = OWN // 2
ROWS = NBO * STATE
TAIL = 32
PAY = ROWS + TAIL
SHARES = NY * NZH
SROWS = ROWS // SHARES
TROWS = SROWS + 8
F32 = jnp.float32
BF16 = jnp.bfloat16
LIMIT = 16 * 1024 * 1024
AXES = ("y", "core", "zh", "zl", "x")
NEAR_AXES = ("zl", "x")
FAR_AXES = ("y", "zh")
SMEM = pl.BlockSpec(memory_space=pltpu.SMEM)
VMEM = pl.BlockSpec(memory_space=pltpu.VMEM)
ANY = pl.BlockSpec(memory_space=pl.ANY)


def params():
    return pltpu.CompilerParams(vmem_limit_bytes=LIMIT)


def three(v):
    hi = v.astype(BF16).astype(F32)
    mid = (v - hi).astype(BF16).astype(F32)
    low = (v - hi - mid).astype(BF16).astype(F32)
    return hi, mid, low


def lanes_of(per_head, base, block, rows):
    lane = lax.broadcasted_iota(jnp.int32, (rows, 128), 1)
    pick = base + 2 * block + lane // HEAD_DIM
    return jnp.take_along_axis(per_head, pick, axis=1)


def prep_kernel(x_hbm, raw_ref, log_ref, x_ref, early_ref, late_ref, sem):
    copy = pltpu.make_async_copy(x_hbm, x_ref, sem)
    copy.start()
    raw = raw_ref[...]
    step = jnp.maximum(raw, 0.0) + jnp.log1p(jnp.exp(-jnp.abs(raw)))
    cum = -jnp.exp(log_ref[...]) * step
    row = lax.broadcasted_iota(jnp.int32, (TOK, HEADS), 0)
    shift = 1
    while shift < TOK:
        cum = cum + jnp.where(row >= shift, pltpu.roll(cum, shift, 0), 0.0)
        shift *= 2
    last = cum[TOK - 1 :, :]
    early_ref[:TOK] = jnp.exp(last - cum) * step
    early_ref[TOK:] = jnp.broadcast_to(jnp.exp(last), (8, HEADS))
    late_ref[:TOK] = cum
    late_ref[TOK : 2 * TOK] = cum.T
    late_ref[2 * TOK :] = step.T
    copy.wait()


def prep(conv_input, step_raw, decay_log):
    channels = conv_input.shape[1]
    return pl.pallas_call(
        prep_kernel,
        in_specs=[ANY, VMEM, VMEM],
        out_specs=[VMEM] * 3,
        out_shape=[
            jax.ShapeDtypeStruct((TOK, channels), BF16),
            jax.ShapeDtypeStruct((TOK + 8, HEADS), F32),
            jax.ShapeDtypeStruct((2 * TOK + HEADS, HEADS), F32),
        ],
        scratch_shapes=[pltpu.SemaphoreType.DMA],
        compiler_params=params(),
        cost_estimate=pl.CostEstimate(flops=0, bytes_accessed=0, transcendentals=0),
    )(conv_input, step_raw, decay_log.reshape(1, HEADS))


def convolve(x_ref, edge_ref, w_ref, at):
    cols = pl.ds(pl.multiple_of(at, 128), 128)
    x = x_ref[:, cols].astype(F32)
    edge = edge_ref[:, cols].astype(F32)
    weight = w_ref[:, cols]
    wide = jnp.concatenate([jnp.zeros((8 - KERNEL + 1, 128), F32), edge, x], 0)
    out = None
    for tap in range(KERNEL):
        first = 8 - KERNEL + 1 + tap
        term = wide[first : first + TOK] * weight[tap : tap + 1]
        out = term if out is None else out + term
    return out.astype(BF16)


def state_kernel(in_ref, edge_ref, w_ref, early_ref, pay_ref):
    factor = early_ref[:TOK]
    decay = early_ref[TOK:]
    blank = jnp.zeros((TAIL - 3 * NBO, 128), F32)
    for group in range(GROUPS):
        writers = convolve(in_ref, edge_ref, w_ref, HCOLS + group * STATE).astype(F32).T.astype(BF16)
        for owner in range(group * PER // OWN, (group + 1) * PER // OWN):
            base = owner * OWN
            rows = [lanes_of(decay, base, b, 8)[:1] for b in range(NBO)]
            terms = three(jnp.concatenate(rows, 0))
            pay_ref[owner, ROWS:] = jnp.concatenate([*terms, blank], 0).astype(BF16)
            for pair in range(NBO // 2):
                weighted = []
                for b in (2 * pair, 2 * pair + 1):
                    value = convolve(in_ref, edge_ref, w_ref, base * HEAD_DIM + b * 128)
                    weighted.append((value.astype(F32) * lanes_of(factor, base, b, TOK)).astype(BF16))
                state = jnp.dot(writers, jnp.concatenate(weighted, 1), preferred_element_type=F32)
                for half in range(2):
                    at = (2 * pair + half) * STATE
                    pay_ref[owner, at : at + STATE] = state[:, half * 128 : (half + 1) * 128].astype(BF16)


def states(*args):
    return pl.pallas_call(
        state_kernel,
        in_specs=[VMEM] * 4,
        out_specs=VMEM,
        out_shape=jax.ShapeDtypeStruct((NEAR, PAY, 128), BF16),
        compiler_params=params(),
        cost_estimate=pl.CostEstimate(flops=10**8, bytes_accessed=3 * 10**6, transcendentals=0),
    )(*args)


def decays_of(ref, source):
    terms = ref[source, ROWS:].astype(F32)
    return terms[:NBO] + terms[NBO : 2 * NBO] + terms[2 * NBO : 3 * NBO]


def total_kernel(pay_ref, out_ref):
    decays = [decays_of(pay_ref, source) for source in range(NEAR)]
    product = decays[0]
    for decay in decays[1:]:
        product = product * decay
    hi, mid, low = three(product)
    for b in range(NBO):
        rows = slice(b * STATE, (b + 1) * STATE)
        total = pay_ref[0, rows].astype(F32)
        for source in range(1, NEAR):
            total = decays[source][b : b + 1] * total + pay_ref[source, rows].astype(F32)
        tail = jnp.concatenate(
            [hi[b : b + 1], mid[b : b + 1], low[b : b + 1], jnp.zeros((5, 128), F32)], 0
        )
        for part in range(STATE // SROWS):
            share = jnp.concatenate([total[part * SROWS : (part + 1) * SROWS], tail], 0)
            out_ref[b * (STATE // SROWS) + part] = share.astype(BF16)


def row_total(pays):
    return pl.pallas_call(
        total_kernel,
        in_specs=[VMEM],
        out_specs=VMEM,
        out_shape=jax.ShapeDtypeStruct((SHARES, TROWS, 128), BF16),
        compiler_params=params(),
    )(pays)


def row_of(rows_ref, at):
    block = rows_ref[at].astype(F32)
    tail = block[SROWS:]
    return block[:SROWS], tail[:1] + tail[1:2] + tail[2:3]


def group_kernel(rows_ref, out_ref):
    for y in range(NY):
        total, product = row_of(rows_ref, y * NZH)
        for z in range(1, NZH):
            state, decay = row_of(rows_ref, y * NZH + z)
            total = decay * total + state
            product = decay * product
        out_ref[y, :SROWS] = total
        out_ref[y, SROWS:] = jnp.broadcast_to(product, (8, 128))


def group_total(rows):
    return pl.pallas_call(
        group_kernel,
        in_specs=[VMEM],
        out_specs=VMEM,
        out_shape=jax.ShapeDtypeStruct((NY, TROWS, 128), F32),
        compiler_params=params(),
    )(rows)


def scan_kernel(core_ref, rows_ref, own_ref, other_ref, out_ref):
    first = core_ref[0] == 0
    entry = jnp.zeros((SROWS, 128), F32)
    for y in range(NY):
        own, other = own_ref[y], other_ref[y]
        one = jnp.where(first, own, other)
        two = jnp.where(first, other, own)
        middle = one[SROWS : SROWS + 1] * entry + one[:SROWS]
        state = jnp.where(first, entry, middle)
        entry = two[SROWS : SROWS + 1] * middle + two[:SROWS]
        for z in range(NZH):
            out_ref[y * NZH + z] = state.astype(BF16)
            if z < NZH - 1:
                term, decay = row_of(rows_ref, y * NZH + z)
                state = decay * state + term


def scan(core, rows, own, other):
    return pl.pallas_call(
        scan_kernel,
        in_specs=[SMEM] + [VMEM] * 3,
        out_specs=VMEM,
        out_shape=jax.ShapeDtypeStruct((SHARES, SROWS, 128), BF16),
        compiler_params=params(),
    )(core, rows, own, other)


def enter_kernel(entry_ref, pay_ref, out_ref):
    decays = [decays_of(pay_ref, source) for source in range(NEAR - 1)]
    for b in range(NBO):
        rows = slice(b * STATE, (b + 1) * STATE)
        state = entry_ref[rows].astype(F32)
        for target in range(NEAR):
            out_ref[target, rows] = state.astype(BF16)
            if target < NEAR - 1:
                state = decays[target][b : b + 1] * state + pay_ref[target, rows].astype(F32)


def enter(entry, pays):
    return pl.pallas_call(
        enter_kernel,
        in_specs=[VMEM] * 2,
        out_specs=VMEM,
        out_shape=jax.ShapeDtypeStruct((NEAR, ROWS, 128), BF16),
        compiler_params=params(),
    )(entry, pays)


def local_kernel(in_ref, edge_ref, w_ref, late_ref, gain_ref, out_ref, rea_ref):
    cum = late_ref[:TOK]
    gain = jnp.broadcast_to(gain_ref[...], (8, HEADS))
    row = lax.broadcasted_iota(jnp.int32, (TOK, TOK), 0)
    col = lax.broadcasted_iota(jnp.int32, (TOK, TOK), 1)
    causal = row >= col
    first = col < HEAD_DIM
    for group in range(GROUPS):
        base = group * PER
        writers = convolve(in_ref, edge_ref, w_ref, HCOLS + group * STATE)
        readers = convolve(in_ref, edge_ref, w_ref, HCOLS + (GROUPS + group) * STATE)
        rea_ref[:, group * STATE : (group + 1) * STATE] = readers
        affinity = lax.dot_general(
            readers, writers, (((1,), (1,)), ((), ())), preferred_element_type=F32
        )
        cum_t = late_ref[TOK + base : TOK + base + PER]
        step_t = late_ref[TOK + HEADS + base : TOK + HEADS + base + PER]
        for b in range(NB):
            scores = []
            for h in (2 * b, 2 * b + 1):
                here = jnp.take_along_axis(cum, jnp.full((TOK, TOK), base + h, jnp.int32), axis=1)
                span = jnp.where(causal, here - cum_t[h : h + 1], -1e30)
                weight = jnp.exp(span) * step_t[h : h + 1]
                scores.append((weight * affinity).astype(BF16))
            at = base * HEAD_DIM + b * 128
            value = convolve(in_ref, edge_ref, w_ref, at)
            zero = jnp.zeros_like(value)
            apart = jnp.concatenate([jnp.where(first, value, zero), jnp.where(first, zero, value)], 0)
            local = jnp.dot(jnp.concatenate(scores, 1), apart, preferred_element_type=F32)
            skip = lanes_of(gain, base, b, 8)[:1]
            out_ref[:, at : at + 128] = local + skip * value.astype(F32)


def local(*args):
    return pl.pallas_call(
        local_kernel,
        in_specs=[VMEM] * 5,
        out_specs=[VMEM] * 2,
        out_shape=[
            jax.ShapeDtypeStruct((TOK, HCOLS), F32),
            jax.ShapeDtypeStruct((TOK, GROUPS * STATE), BF16),
        ],
        compiler_params=params(),
        cost_estimate=pl.CostEstimate(flops=10**9, bytes_accessed=8 * 10**6, transcendentals=0),
    )(*args)


def final_kernel(rea_ref, late_ref, part_ref, state_ref, out_ref, buf, sems):
    growth = jnp.exp(late_ref[:TOK])
    width = OWN * HEAD_DIM
    copies = []
    for owner in range(NEAR):
        base = owner * OWN
        group = base // PER
        readers = rea_ref[:, group * STATE : (group + 1) * STATE]
        for pair in range(NBO // 2):
            at = 2 * pair * STATE
            both = jnp.concatenate(
                [state_ref[owner, at : at + STATE], state_ref[owner, at + STATE : at + 2 * STATE]], 1
            )
            carried = jnp.dot(readers, both, preferred_element_type=F32)
            for half in range(2):
                b = 2 * pair + half
                cols = slice(owner * width + b * 128, owner * width + (b + 1) * 128)
                grow = lanes_of(growth, base, b, TOK)
                result = part_ref[:, cols] + carried[:, half * 128 : (half + 1) * 128] * grow
                buf[:, cols] = result.astype(BF16)
        cols = pl.ds(owner * width, width)
        copies.append(pltpu.make_async_copy(buf.at[:, cols], out_ref.at[:, cols], sems.at[owner]))
        copies[-1].start()
    for copy in copies:
        copy.wait()


def final(*args):
    return pl.pallas_call(
        final_kernel,
        in_specs=[VMEM] * 4,
        out_specs=ANY,
        out_shape=jax.ShapeDtypeStruct((TOK, HCOLS), BF16),
        scratch_shapes=[pltpu.VMEM((TOK, HCOLS), BF16), pltpu.SemaphoreType.DMA((NEAR,))],
        compiler_params=params(),
        cost_estimate=pl.CostEstimate(flops=10**8, bytes_accessed=2 * 10**6, transcendentals=0),
    )(*args)


def body(conv_input, conv_weight, step_raw, decay_log, skip_gain):
    count = lax.axis_size(AXES)
    core = lax.axis_index("core").reshape(1)
    edge = lax.ppermute(conv_input[TOK - KERNEL + 1 :], AXES, [(i, i + 1) for i in range(count - 1)])
    held, early, late = prep(conv_input, step_raw, decay_log)
    made = states(held, edge, conv_weight, early)
    pays = lax.all_to_all(made, NEAR_AXES, 0, 0, tiled=True)
    rows = lax.all_to_all(row_total(pays), FAR_AXES, 0, 0, tiled=True)
    own = group_total(rows)
    other = lax.ppermute(own, "core", [(0, 1), (1, 0)])
    entry = lax.all_to_all(scan(core, rows, own, other), FAR_AXES, 0, 0, tiled=True)
    entering = enter(entry.reshape(ROWS, 128), pays)
    late, entering = lax.optimization_barrier((late, entering))
    state = lax.all_to_all(entering, NEAR_AXES, 0, 0, tiled=True)
    part, readers = local(conv_input, edge, conv_weight, late, skip_gain.reshape(1, HEADS))
    return final(readers, late, part, state)


def solution(mesh):
    fine = Mesh(mesh.devices.reshape(NY, 2, NZH, NZL, NX), AXES)
    in_specs = (P(AXES, None), P(), P(AXES, None), P(), P())
    return jax.shard_map(body, mesh=fine, in_specs=in_specs, out_specs=P(AXES, None), check_vma=False)
```

```python
import jax
import jax.numpy as jnp
from jax import lax
from jax.experimental import pallas as pl
from jax.experimental.pallas import tpu as pltpu
from jax.sharding import Mesh, PartitionSpec as P

HEADS = 128
HEAD_DIM = 64
STATE = 128
GROUPS = 4
KERNEL = 4
TOK = 128
PER = HEADS // GROUPS
NB = PER // 2
HCOLS = HEADS * HEAD_DIM
NX, NY, NZ = 4, 8, 8
NZL = 2
NZH = NZ // NZL
NEAR = NZL * NX
OWN = HEADS // NEAR
NBO = OWN // 2
ROWS = NBO * STATE
TAIL = 32
PAY = ROWS + TAIL
SHARES = NY * NZH
SROWS = ROWS // SHARES
TROWS = SROWS + 8
F32 = jnp.float32
BF16 = jnp.bfloat16
LIMIT = 16 * 1024 * 1024
AXES = ("y", "core", "zh", "zl", "x")
NEAR_AXES = ("zl", "x")
FAR_AXES = ("y", "zh")
SMEM = pl.BlockSpec(memory_space=pltpu.SMEM)
VMEM = pl.BlockSpec(memory_space=pltpu.VMEM)
ANY = pl.BlockSpec(memory_space=pl.ANY)


def params():
    return pltpu.CompilerParams(vmem_limit_bytes=LIMIT)


def three(v):
    hi = v.astype(BF16).astype(F32)
    mid = (v - hi).astype(BF16).astype(F32)
    low = (v - hi - mid).astype(BF16).astype(F32)
    return hi, mid, low


def lanes_of(per_head, base, block, rows):
    lane = lax.broadcasted_iota(jnp.int32, (rows, 128), 1)
    pick = base + 2 * block + lane // HEAD_DIM
    return jnp.take_along_axis(per_head, pick, axis=1)


def prep_kernel(x_hbm, raw_ref, log_ref, x_ref, early_ref, late_ref, sem):
    copy = pltpu.make_async_copy(x_hbm, x_ref, sem)
    copy.start()
    raw = raw_ref[...]
    step = jnp.maximum(raw, 0.0) + jnp.log1p(jnp.exp(-jnp.abs(raw)))
    cum = -jnp.exp(log_ref[...]) * step
    row = lax.broadcasted_iota(jnp.int32, (TOK, HEADS), 0)
    shift = 1
    while shift < TOK:
        cum = cum + jnp.where(row >= shift, pltpu.roll(cum, shift, 0), 0.0)
        shift *= 2
    last = cum[TOK - 1 :, :]
    early_ref[:TOK] = jnp.exp(last - cum) * step
    early_ref[TOK:] = jnp.broadcast_to(jnp.exp(last), (8, HEADS))
    late_ref[:TOK] = cum
    late_ref[TOK : 2 * TOK] = cum.T
    late_ref[2 * TOK :] = step.T
    copy.wait()


def prep(conv_input, step_raw, decay_log):
    channels = conv_input.shape[1]
    return pl.pallas_call(
        prep_kernel,
        in_specs=[ANY, VMEM, VMEM],
        out_specs=[VMEM] * 3,
        out_shape=[
            jax.ShapeDtypeStruct((TOK, channels), BF16),
            jax.ShapeDtypeStruct((TOK + 8, HEADS), F32),
            jax.ShapeDtypeStruct((2 * TOK + HEADS, HEADS), F32),
        ],
        scratch_shapes=[pltpu.SemaphoreType.DMA],
        compiler_params=params(),
        cost_estimate=pl.CostEstimate(flops=0, bytes_accessed=0, transcendentals=0),
    )(conv_input, step_raw, decay_log.reshape(1, HEADS))


def convolve(x_ref, edge_ref, w_ref, at):
    cols = pl.ds(pl.multiple_of(at, 128), 128)
    x = x_ref[:, cols].astype(F32)
    edge = edge_ref[:, cols].astype(F32)
    weight = w_ref[:, cols]
    wide = jnp.concatenate([jnp.zeros((8 - KERNEL + 1, 128), F32), edge, x], 0)
    out = None
    for tap in range(KERNEL):
        first = 8 - KERNEL + 1 + tap
        term = wide[first : first + TOK] * weight[tap : tap + 1]
        out = term if out is None else out + term
    return out.astype(BF16)


SLOTS = 4


def convolve_by_loads(x_ref, edge_ref, w_ref, at, wide_ref):
    cols = slice(at, at + 128)
    wide_ref[8 - KERNEL + 1 : 8] = edge_ref[:, cols].astype(F32)
    wide_ref[8:] = x_ref[:, cols].astype(F32)
    out = None
    for tap in range(KERNEL):
        first = 8 - KERNEL + 1 + tap
        term = wide_ref[first : first + TOK] * w_ref[tap : tap + 1, cols]
        out = term if out is None else out + term
    return out.astype(BF16)


def state_kernel(in_ref, edge_ref, w_ref, early_ref, pay_ref, wide_ref):
    factor = early_ref[:TOK]
    decay = early_ref[TOK:]
    blank = jnp.zeros((TAIL - 3 * NBO, 128), F32)
    for group in range(GROUPS):
        writers = convolve_by_loads(in_ref, edge_ref, w_ref, HCOLS + group * STATE, wide_ref.at[0]).astype(F32).T.astype(BF16)
        for owner in range(group * PER // OWN, (group + 1) * PER // OWN):
            base = owner * OWN
            rows = [lanes_of(decay, base, b, 8)[:1] for b in range(NBO)]
            terms = three(jnp.concatenate(rows, 0))
            pay_ref[owner, ROWS:] = jnp.concatenate([*terms, blank], 0).astype(BF16)
            for pair in range(NBO // 2):
                weighted = []
                for b in (2 * pair, 2 * pair + 1):
                    value = convolve_by_loads(
                        in_ref, edge_ref, w_ref, base * HEAD_DIM + b * 128, wide_ref.at[b % SLOTS]
                    )
                    weighted.append((value.astype(F32) * lanes_of(factor, base, b, TOK)).astype(BF16))
                state = jnp.dot(writers, jnp.concatenate(weighted, 1), preferred_element_type=F32)
                for half in range(2):
                    at = (2 * pair + half) * STATE
                    pay_ref[owner, at : at + STATE] = state[:, half * 128 : (half + 1) * 128].astype(BF16)


def states(*args):
    return pl.pallas_call(
        state_kernel,
        in_specs=[VMEM] * 4,
        out_specs=VMEM,
        out_shape=jax.ShapeDtypeStruct((NEAR, PAY, 128), BF16),
        scratch_shapes=[pltpu.VMEM((SLOTS, TOK + 8, 128), F32)],
        compiler_params=params(),
        cost_estimate=pl.CostEstimate(flops=10**8, bytes_accessed=3 * 10**6, transcendentals=0),
    )(*args)


def decays_of(ref, source):
    terms = ref[source, ROWS:].astype(F32)
    return terms[:NBO] + terms[NBO : 2 * NBO] + terms[2 * NBO : 3 * NBO]


def total_kernel(pay_ref, out_ref):
    decays = [decays_of(pay_ref, source) for source in range(NEAR)]
    product = decays[0]
    for decay in decays[1:]:
        product = product * decay
    hi, mid, low = three(product)
    for b in range(NBO):
        rows = slice(b * STATE, (b + 1) * STATE)
        total = pay_ref[0, rows].astype(F32)
        for source in range(1, NEAR):
            total = decays[source][b : b + 1] * total + pay_ref[source, rows].astype(F32)
        tail = jnp.concatenate(
            [hi[b : b + 1], mid[b : b + 1], low[b : b + 1], jnp.zeros((5, 128), F32)], 0
        )
        for part in range(STATE // SROWS):
            share = jnp.concatenate([total[part * SROWS : (part + 1) * SROWS], tail], 0)
            out_ref[b * (STATE // SROWS) + part] = share.astype(BF16)


def row_total(pays):
    return pl.pallas_call(
        total_kernel,
        in_specs=[VMEM],
        out_specs=VMEM,
        out_shape=jax.ShapeDtypeStruct((SHARES, TROWS, 128), BF16),
        compiler_params=params(),
    )(pays)


def row_of(rows_ref, at):
    block = rows_ref[at].astype(F32)
    tail = block[SROWS:]
    return block[:SROWS], tail[:1] + tail[1:2] + tail[2:3]


def group_kernel(rows_ref, out_ref):
    for y in range(NY):
        total, product = row_of(rows_ref, y * NZH)
        for z in range(1, NZH):
            state, decay = row_of(rows_ref, y * NZH + z)
            total = decay * total + state
            product = decay * product
        out_ref[y, :SROWS] = total
        out_ref[y, SROWS:] = jnp.broadcast_to(product, (8, 128))


def group_total(rows):
    return pl.pallas_call(
        group_kernel,
        in_specs=[VMEM],
        out_specs=VMEM,
        out_shape=jax.ShapeDtypeStruct((NY, TROWS, 128), F32),
        compiler_params=params(),
    )(rows)


def scan_kernel(core_ref, rows_ref, own_ref, other_ref, out_ref):
    first = core_ref[0] == 0
    entry = jnp.zeros((SROWS, 128), F32)
    for y in range(NY):
        own, other = own_ref[y], other_ref[y]
        one = jnp.where(first, own, other)
        two = jnp.where(first, other, own)
        middle = one[SROWS : SROWS + 1] * entry + one[:SROWS]
        state = jnp.where(first, entry, middle)
        entry = two[SROWS : SROWS + 1] * middle + two[:SROWS]
        for z in range(NZH):
            out_ref[y * NZH + z] = state.astype(BF16)
            if z < NZH - 1:
                term, decay = row_of(rows_ref, y * NZH + z)
                state = decay * state + term


def scan(core, rows, own, other):
    return pl.pallas_call(
        scan_kernel,
        in_specs=[SMEM] + [VMEM] * 3,
        out_specs=VMEM,
        out_shape=jax.ShapeDtypeStruct((SHARES, SROWS, 128), BF16),
        compiler_params=params(),
    )(core, rows, own, other)


def enter_kernel(entry_ref, pay_ref, out_ref):
    decays = [decays_of(pay_ref, source) for source in range(NEAR - 1)]
    for b in range(NBO):
        rows = slice(b * STATE, (b + 1) * STATE)
        state = entry_ref[rows].astype(F32)
        for target in range(NEAR):
            out_ref[target, rows] = state.astype(BF16)
            if target < NEAR - 1:
                state = decays[target][b : b + 1] * state + pay_ref[target, rows].astype(F32)


def enter(entry, pays):
    return pl.pallas_call(
        enter_kernel,
        in_specs=[VMEM] * 2,
        out_specs=VMEM,
        out_shape=jax.ShapeDtypeStruct((NEAR, ROWS, 128), BF16),
        compiler_params=params(),
    )(entry, pays)


def local_kernel(in_ref, edge_ref, w_ref, late_ref, gain_ref, out_ref, rea_ref):
    cum = late_ref[:TOK]
    gain = jnp.broadcast_to(gain_ref[...], (8, HEADS))
    row = lax.broadcasted_iota(jnp.int32, (TOK, TOK), 0)
    col = lax.broadcasted_iota(jnp.int32, (TOK, TOK), 1)
    causal = row >= col
    first = col < HEAD_DIM
    for group in range(GROUPS):
        base = group * PER
        writers = convolve(in_ref, edge_ref, w_ref, HCOLS + group * STATE)
        readers = convolve(in_ref, edge_ref, w_ref, HCOLS + (GROUPS + group) * STATE)
        rea_ref[:, group * STATE : (group + 1) * STATE] = readers
        affinity = lax.dot_general(
            readers, writers, (((1,), (1,)), ((), ())), preferred_element_type=F32
        )
        cum_t = late_ref[TOK + base : TOK + base + PER]
        step_t = late_ref[TOK + HEADS + base : TOK + HEADS + base + PER]
        for b in range(NB):
            scores = []
            for h in (2 * b, 2 * b + 1):
                here = jnp.take_along_axis(cum, jnp.full((TOK, TOK), base + h, jnp.int32), axis=1)
                span = jnp.where(causal, here - cum_t[h : h + 1], -1e30)
                weight = jnp.exp(span) * step_t[h : h + 1]
                scores.append((weight * affinity).astype(BF16))
            at = base * HEAD_DIM + b * 128
            value = convolve(in_ref, edge_ref, w_ref, at)
            zero = jnp.zeros_like(value)
            apart = jnp.concatenate([jnp.where(first, value, zero), jnp.where(first, zero, value)], 0)
            local = jnp.dot(jnp.concatenate(scores, 1), apart, preferred_element_type=F32)
            skip = lanes_of(gain, base, b, 8)[:1]
            out_ref[:, at : at + 128] = local + skip * value.astype(F32)


def local(*args):
    return pl.pallas_call(
        local_kernel,
        in_specs=[VMEM] * 5,
        out_specs=[VMEM] * 2,
        out_shape=[
            jax.ShapeDtypeStruct((TOK, HCOLS), F32),
            jax.ShapeDtypeStruct((TOK, GROUPS * STATE), BF16),
        ],
        compiler_params=params(),
        cost_estimate=pl.CostEstimate(flops=10**9, bytes_accessed=8 * 10**6, transcendentals=0),
    )(*args)


def final_kernel(rea_ref, late_ref, part_ref, state_ref, out_ref, buf, sems):
    growth = jnp.exp(late_ref[:TOK])
    width = OWN * HEAD_DIM
    copies = []
    for owner in range(NEAR):
        base = owner * OWN
        group = base // PER
        readers = rea_ref[:, group * STATE : (group + 1) * STATE]
        for pair in range(NBO // 2):
            at = 2 * pair * STATE
            both = jnp.concatenate(
                [state_ref[owner, at : at + STATE], state_ref[owner, at + STATE : at + 2 * STATE]], 1
            )
            carried = jnp.dot(readers, both, preferred_element_type=F32)
            for half in range(2):
                b = 2 * pair + half
                cols = slice(owner * width + b * 128, owner * width + (b + 1) * 128)
                grow = lanes_of(growth, base, b, TOK)
                result = part_ref[:, cols] + carried[:, half * 128 : (half + 1) * 128] * grow
                buf[:, cols] = result.astype(BF16)
        cols = pl.ds(owner * width, width)
        copies.append(pltpu.make_async_copy(buf.at[:, cols], out_ref.at[:, cols], sems.at[owner]))
        copies[-1].start()
    for copy in copies:
        copy.wait()


def final(*args):
    return pl.pallas_call(
        final_kernel,
        in_specs=[VMEM] * 4,
        out_specs=ANY,
        out_shape=jax.ShapeDtypeStruct((TOK, HCOLS), BF16),
        scratch_shapes=[pltpu.VMEM((TOK, HCOLS), BF16), pltpu.SemaphoreType.DMA((NEAR,))],
        compiler_params=params(),
        cost_estimate=pl.CostEstimate(flops=10**8, bytes_accessed=2 * 10**6, transcendentals=0),
    )(*args)


def body(conv_input, conv_weight, step_raw, decay_log, skip_gain):
    count = lax.axis_size(AXES)
    core = lax.axis_index("core").reshape(1)
    edge = lax.ppermute(conv_input[TOK - KERNEL + 1 :], AXES, [(i, i + 1) for i in range(count - 1)])
    held, early, late = prep(conv_input, step_raw, decay_log)
    made = states(held, edge, conv_weight, early)
    pays = lax.all_to_all(made, NEAR_AXES, 0, 0, tiled=True)
    part, readers = local(conv_input, edge, conv_weight, late, skip_gain.reshape(1, HEADS))
    pays, part, readers = lax.optimization_barrier((pays, part, readers))
    rows = lax.all_to_all(row_total(pays), FAR_AXES, 0, 0, tiled=True)
    own = group_total(rows)
    other = lax.ppermute(own, "core", [(0, 1), (1, 0)])
    entry = lax.all_to_all(scan(core, rows, own, other), FAR_AXES, 0, 0, tiled=True)
    entering = enter(entry.reshape(ROWS, 128), pays)
    state = lax.all_to_all(entering, NEAR_AXES, 0, 0, tiled=True)
    return final(readers, late, part, state)


def solution(mesh):
    fine = Mesh(mesh.devices.reshape(NY, 2, NZH, NZL, NX), AXES)
    in_specs = (P(AXES, None), P(), P(AXES, None), P(), P())
    return jax.shard_map(body, mesh=fine, in_specs=in_specs, out_specs=P(AXES, None), check_vma=False)
```

```python
import jax
import jax.numpy as jnp
from jax import lax
from jax.experimental import pallas as pl
from jax.experimental.pallas import tpu as pltpu
from jax.sharding import Mesh, PartitionSpec as P

HEADS = 128
HEAD_DIM = 64
STATE = 128
GROUPS = 4
KERNEL = 4
TOK = 128
PER = HEADS // GROUPS
NB = PER // 2
HCOLS = HEADS * HEAD_DIM
NX, NY, NZ = 4, 8, 8
NZL = 2
NZH = NZ // NZL
NEAR = NZL * NX
OWN = HEADS // NEAR
NBO = OWN // 2
ROWS = NBO * STATE
TAIL = 32
PAY = ROWS + TAIL
SHARES = NY * NZH
SROWS = ROWS // SHARES
TROWS = SROWS + 8
F32 = jnp.float32
BF16 = jnp.bfloat16
LIMIT = 16 * 1024 * 1024
AXES = ("y", "core", "zh", "zl", "x")
NEAR_AXES = ("zl", "x")
FAR_AXES = ("y", "zh")
SMEM = pl.BlockSpec(memory_space=pltpu.SMEM)
VMEM = pl.BlockSpec(memory_space=pltpu.VMEM)
ANY = pl.BlockSpec(memory_space=pl.ANY)


def params():
    return pltpu.CompilerParams(vmem_limit_bytes=LIMIT)


def three(v):
    hi = v.astype(BF16).astype(F32)
    mid = (v - hi).astype(BF16).astype(F32)
    low = (v - hi - mid).astype(BF16).astype(F32)
    return hi, mid, low


def lanes_of(per_head, base, block, rows):
    lane = lax.broadcasted_iota(jnp.int32, (rows, 128), 1)
    pick = base + 2 * block + lane // HEAD_DIM
    return jnp.take_along_axis(per_head, pick, axis=1)


def prep_kernel(x_hbm, raw_ref, log_ref, x_ref, early_ref, late_ref, sem):
    copy = pltpu.make_async_copy(x_hbm, x_ref, sem)
    copy.start()
    raw = raw_ref[...]
    step = jnp.maximum(raw, 0.0) + jnp.log1p(jnp.exp(-jnp.abs(raw)))
    cum = -jnp.exp(log_ref[...]) * step
    row = lax.broadcasted_iota(jnp.int32, (TOK, HEADS), 0)
    shift = 1
    while shift < TOK:
        cum = cum + jnp.where(row >= shift, pltpu.roll(cum, shift, 0), 0.0)
        shift *= 2
    last = cum[TOK - 1 :, :]
    early_ref[:TOK] = jnp.exp(last - cum) * step
    early_ref[TOK:] = jnp.broadcast_to(jnp.exp(last), (8, HEADS))
    late_ref[:TOK] = cum
    late_ref[TOK : 2 * TOK] = cum.T
    late_ref[2 * TOK :] = step.T
    copy.wait()


def prep(conv_input, step_raw, decay_log):
    channels = conv_input.shape[1]
    return pl.pallas_call(
        prep_kernel,
        in_specs=[ANY, VMEM, VMEM],
        out_specs=[VMEM] * 3,
        out_shape=[
            jax.ShapeDtypeStruct((TOK, channels), BF16),
            jax.ShapeDtypeStruct((TOK + 8, HEADS), F32),
            jax.ShapeDtypeStruct((2 * TOK + HEADS, HEADS), F32),
        ],
        scratch_shapes=[pltpu.SemaphoreType.DMA],
        compiler_params=params(),
        cost_estimate=pl.CostEstimate(flops=0, bytes_accessed=0, transcendentals=0),
    )(conv_input, step_raw, decay_log.reshape(1, HEADS))


def convolve(x_ref, edge_ref, w_ref, at):
    cols = pl.ds(pl.multiple_of(at, 128), 128)
    x = x_ref[:, cols].astype(F32)
    edge = edge_ref[:, cols].astype(F32)
    weight = w_ref[:, cols]
    wide = jnp.concatenate([jnp.zeros((8 - KERNEL + 1, 128), F32), edge, x], 0)
    out = None
    for tap in range(KERNEL):
        first = 8 - KERNEL + 1 + tap
        term = wide[first : first + TOK] * weight[tap : tap + 1]
        out = term if out is None else out + term
    return out.astype(BF16)


SLOTS = 4


def convolve_by_loads(x_ref, edge_ref, w_ref, at, wide_ref):
    cols = slice(at, at + 128)
    wide_ref[8 - KERNEL + 1 : 8] = edge_ref[:, cols].astype(F32)
    wide_ref[8:] = x_ref[:, cols].astype(F32)
    out = None
    for tap in range(KERNEL):
        first = 8 - KERNEL + 1 + tap
        term = wide_ref[first : first + TOK] * w_ref[tap : tap + 1, cols]
        out = term if out is None else out + term
    return out.astype(BF16)


def state_kernel(in_ref, edge_ref, w_ref, early_ref, pay_ref, wide_ref):
    factor = early_ref[:TOK]
    decay = early_ref[TOK:]
    blank = jnp.zeros((TAIL - 3 * NBO, 128), F32)
    for group in range(GROUPS):
        writers = convolve_by_loads(in_ref, edge_ref, w_ref, HCOLS + group * STATE, wide_ref.at[0]).astype(F32).T.astype(BF16)
        for owner in range(group * PER // OWN, (group + 1) * PER // OWN):
            base = owner * OWN
            rows = [lanes_of(decay, base, b, 8)[:1] for b in range(NBO)]
            terms = three(jnp.concatenate(rows, 0))
            pay_ref[owner, ROWS:] = jnp.concatenate([*terms, blank], 0).astype(BF16)
            for pair in range(NBO // 2):
                weighted = []
                for b in (2 * pair, 2 * pair + 1):
                    value = convolve_by_loads(
                        in_ref, edge_ref, w_ref, base * HEAD_DIM + b * 128, wide_ref.at[b % SLOTS]
                    )
                    weighted.append((value.astype(F32) * lanes_of(factor, base, b, TOK)).astype(BF16))
                state = jnp.dot(writers, jnp.concatenate(weighted, 1), preferred_element_type=F32)
                for half in range(2):
                    at = (2 * pair + half) * STATE
                    pay_ref[owner, at : at + STATE] = state[:, half * 128 : (half + 1) * 128].astype(BF16)


def states(*args):
    return pl.pallas_call(
        state_kernel,
        in_specs=[VMEM] * 4,
        out_specs=VMEM,
        out_shape=jax.ShapeDtypeStruct((NEAR, PAY, 128), BF16),
        scratch_shapes=[pltpu.VMEM((SLOTS, TOK + 8, 128), F32)],
        compiler_params=params(),
        cost_estimate=pl.CostEstimate(flops=10**8, bytes_accessed=3 * 10**6, transcendentals=0),
    )(*args)


def decays_of(ref, source):
    terms = ref[source, ROWS:].astype(F32)
    return terms[:NBO] + terms[NBO : 2 * NBO] + terms[2 * NBO : 3 * NBO]


def total_kernel(pay_ref, out_ref):
    decays = [decays_of(pay_ref, source) for source in range(NEAR)]
    product = decays[0]
    for decay in decays[1:]:
        product = product * decay
    hi, mid, low = three(product)
    for b in range(NBO):
        rows = slice(b * STATE, (b + 1) * STATE)
        total = pay_ref[0, rows].astype(F32)
        for source in range(1, NEAR):
            total = decays[source][b : b + 1] * total + pay_ref[source, rows].astype(F32)
        tail = jnp.concatenate(
            [hi[b : b + 1], mid[b : b + 1], low[b : b + 1], jnp.zeros((5, 128), F32)], 0
        )
        for part in range(STATE // SROWS):
            share = jnp.concatenate([total[part * SROWS : (part + 1) * SROWS], tail], 0)
            out_ref[b * (STATE // SROWS) + part] = share.astype(BF16)


def row_total(pays):
    return pl.pallas_call(
        total_kernel,
        in_specs=[VMEM],
        out_specs=VMEM,
        out_shape=jax.ShapeDtypeStruct((SHARES, TROWS, 128), BF16),
        compiler_params=params(),
    )(pays)


def row_of(rows_ref, at):
    block = rows_ref[at].astype(F32)
    tail = block[SROWS:]
    return block[:SROWS], tail[:1] + tail[1:2] + tail[2:3]


def group_kernel(rows_ref, out_ref):
    for y in range(NY):
        total, product = row_of(rows_ref, y * NZH)
        for z in range(1, NZH):
            state, decay = row_of(rows_ref, y * NZH + z)
            total = decay * total + state
            product = decay * product
        out_ref[y, :SROWS] = total
        out_ref[y, SROWS:] = jnp.broadcast_to(product, (8, 128))


def group_total(rows):
    return pl.pallas_call(
        group_kernel,
        in_specs=[VMEM],
        out_specs=VMEM,
        out_shape=jax.ShapeDtypeStruct((NY, TROWS, 128), F32),
        compiler_params=params(),
    )(rows)


def scan_kernel(core_ref, rows_ref, own_ref, other_ref, out_ref):
    first = core_ref[0] == 0
    entry = jnp.zeros((SROWS, 128), F32)
    for y in range(NY):
        own, other = own_ref[y], other_ref[y]
        one = jnp.where(first, own, other)
        two = jnp.where(first, other, own)
        middle = one[SROWS : SROWS + 1] * entry + one[:SROWS]
        state = jnp.where(first, entry, middle)
        entry = two[SROWS : SROWS + 1] * middle + two[:SROWS]
        for z in range(NZH):
            out_ref[y * NZH + z] = state.astype(BF16)
            if z < NZH - 1:
                term, decay = row_of(rows_ref, y * NZH + z)
                state = decay * state + term


def scan(core, rows, own, other):
    return pl.pallas_call(
        scan_kernel,
        in_specs=[SMEM] + [VMEM] * 3,
        out_specs=VMEM,
        out_shape=jax.ShapeDtypeStruct((SHARES, SROWS, 128), BF16),
        compiler_params=params(),
    )(core, rows, own, other)


def enter_kernel(entry_ref, pay_ref, out_ref):
    decays = [decays_of(pay_ref, source) for source in range(NEAR - 1)]
    for b in range(NBO):
        rows = slice(b * STATE, (b + 1) * STATE)
        state = entry_ref[rows].astype(F32)
        for target in range(NEAR):
            out_ref[target, rows] = state.astype(BF16)
            if target < NEAR - 1:
                state = decays[target][b : b + 1] * state + pay_ref[target, rows].astype(F32)


def enter(entry, pays):
    return pl.pallas_call(
        enter_kernel,
        in_specs=[VMEM] * 2,
        out_specs=VMEM,
        out_shape=jax.ShapeDtypeStruct((NEAR, ROWS, 128), BF16),
        compiler_params=params(),
    )(entry, pays)


def local_kernel(in_ref, edge_ref, w_ref, late_ref, gain_ref, out_ref, rea_ref):
    cum = late_ref[:TOK]
    gain = jnp.broadcast_to(gain_ref[...], (8, HEADS))
    row = lax.broadcasted_iota(jnp.int32, (TOK, TOK), 0)
    col = lax.broadcasted_iota(jnp.int32, (TOK, TOK), 1)
    causal = row >= col
    first = col < HEAD_DIM
    for group in range(GROUPS):
        base = group * PER
        writers = convolve(in_ref, edge_ref, w_ref, HCOLS + group * STATE)
        readers = convolve(in_ref, edge_ref, w_ref, HCOLS + (GROUPS + group) * STATE)
        rea_ref[:, group * STATE : (group + 1) * STATE] = readers
        affinity = lax.dot_general(
            readers, writers, (((1,), (1,)), ((), ())), preferred_element_type=F32
        )
        cum_t = late_ref[TOK + base : TOK + base + PER]
        step_t = late_ref[TOK + HEADS + base : TOK + HEADS + base + PER]
        for b in range(NB):
            scores = []
            for h in (2 * b, 2 * b + 1):
                here = jnp.take_along_axis(cum, jnp.full((TOK, TOK), base + h, jnp.int32), axis=1)
                span = jnp.where(causal, here - cum_t[h : h + 1], -1e30)
                weight = jnp.exp(span) * step_t[h : h + 1]
                scores.append((weight * affinity).astype(BF16))
            at = base * HEAD_DIM + b * 128
            value = convolve(in_ref, edge_ref, w_ref, at)
            zero = jnp.zeros_like(value)
            apart = jnp.concatenate([jnp.where(first, value, zero), jnp.where(first, zero, value)], 0)
            local = jnp.dot(jnp.concatenate(scores, 1), apart, preferred_element_type=F32)
            skip = lanes_of(gain, base, b, 8)[:1]
            out_ref[:, at : at + 128] = local + skip * value.astype(F32)


def local(*args):
    return pl.pallas_call(
        local_kernel,
        in_specs=[VMEM] * 5,
        out_specs=[VMEM] * 2,
        out_shape=[
            jax.ShapeDtypeStruct((TOK, HCOLS), F32),
            jax.ShapeDtypeStruct((TOK, GROUPS * STATE), BF16),
        ],
        compiler_params=params(),
        cost_estimate=pl.CostEstimate(flops=10**9, bytes_accessed=8 * 10**6, transcendentals=0),
    )(*args)


def final_kernel(rea_ref, late_ref, part_ref, state_ref, out_ref, buf, sems):
    growth = jnp.exp(late_ref[:TOK])
    width = OWN * HEAD_DIM
    copies = []
    for owner in range(NEAR):
        base = owner * OWN
        group = base // PER
        readers = rea_ref[:, group * STATE : (group + 1) * STATE]
        for pair in range(NBO // 2):
            at = 2 * pair * STATE
            both = jnp.concatenate(
                [state_ref[owner, at : at + STATE], state_ref[owner, at + STATE : at + 2 * STATE]], 1
            )
            carried = jnp.dot(readers, both, preferred_element_type=F32)
            for half in range(2):
                b = 2 * pair + half
                cols = slice(owner * width + b * 128, owner * width + (b + 1) * 128)
                grow = lanes_of(growth, base, b, TOK)
                result = part_ref[:, cols] + carried[:, half * 128 : (half + 1) * 128] * grow
                buf[:, cols] = result.astype(BF16)
        cols = pl.ds(owner * width, width)
        copies.append(pltpu.make_async_copy(buf.at[:, cols], out_ref.at[:, cols], sems.at[owner]))
        copies[-1].start()
    for copy in copies:
        copy.wait()


def final(*args):
    return pl.pallas_call(
        final_kernel,
        in_specs=[VMEM] * 4,
        out_specs=ANY,
        out_shape=jax.ShapeDtypeStruct((TOK, HCOLS), BF16),
        scratch_shapes=[pltpu.VMEM((TOK, HCOLS), BF16), pltpu.SemaphoreType.DMA((NEAR,))],
        compiler_params=params(),
        cost_estimate=pl.CostEstimate(flops=10**8, bytes_accessed=2 * 10**6, transcendentals=0),
    )(*args)


def body(conv_input, conv_weight, step_raw, decay_log, skip_gain):
    count = lax.axis_size(AXES)
    core = lax.axis_index("core").reshape(1)
    edge = lax.ppermute(conv_input[TOK - KERNEL + 1 :], AXES, [(i, i + 1) for i in range(count - 1)])
    held, early, late = prep(conv_input, step_raw, decay_log)
    made = states(held, edge, conv_weight, early)
    pays = lax.all_to_all(made, NEAR_AXES, 0, 0, tiled=True)
    late, pays = lax.optimization_barrier((late, pays))
    rows = lax.all_to_all(row_total(pays), FAR_AXES, 0, 0, tiled=True)
    part, readers = local(conv_input, edge, conv_weight, late, skip_gain.reshape(1, HEADS))
    rows, part, readers = lax.optimization_barrier((rows, part, readers))
    own = group_total(rows)
    other = lax.ppermute(own, "core", [(0, 1), (1, 0)])
    entry = lax.all_to_all(scan(core, rows, own, other), FAR_AXES, 0, 0, tiled=True)
    entering = enter(entry.reshape(ROWS, 128), pays)
    state = lax.all_to_all(entering, NEAR_AXES, 0, 0, tiled=True)
    return final(readers, late, part, state)


def solution(mesh):
    fine = Mesh(mesh.devices.reshape(NY, 2, NZH, NZL, NX), AXES)
    in_specs = (P(AXES, None), P(), P(AXES, None), P(), P())
    return jax.shard_map(body, mesh=fine, in_specs=in_specs, out_specs=P(AXES, None), check_vma=False)
```

```python
import jax
import jax.numpy as jnp
from jax import lax
from jax.experimental import pallas as pl
from jax.experimental.pallas import tpu as pltpu
from jax.sharding import Mesh, PartitionSpec as P

HEADS = 128
HEAD_DIM = 64
STATE = 128
GROUPS = 4
KERNEL = 4
TOK = 128
PER = HEADS // GROUPS
NB = PER // 2
HCOLS = HEADS * HEAD_DIM
NX, NY, NZ = 4, 8, 8
NZL = 2
NZH = NZ // NZL
NEAR = NZL * NX
OWN = HEADS // NEAR
NBO = OWN // 2
ROWS = NBO * STATE
TAIL = 32
PAY = ROWS + TAIL
SHARES = NY * NZH
SROWS = ROWS // SHARES
TROWS = SROWS + 8
F32 = jnp.float32
BF16 = jnp.bfloat16
LIMIT = 16 * 1024 * 1024
AXES = ("y", "core", "zh", "zl", "x")
NEAR_AXES = ("zl", "x")
FAR_AXES = ("y", "zh")
SMEM = pl.BlockSpec(memory_space=pltpu.SMEM)
VMEM = pl.BlockSpec(memory_space=pltpu.VMEM)
ANY = pl.BlockSpec(memory_space=pl.ANY)


def params():
    return pltpu.CompilerParams(vmem_limit_bytes=LIMIT)


def three(v):
    hi = v.astype(BF16).astype(F32)
    mid = (v - hi).astype(BF16).astype(F32)
    low = (v - hi - mid).astype(BF16).astype(F32)
    return hi, mid, low


def lanes_of(per_head, base, block, rows):
    lane = lax.broadcasted_iota(jnp.int32, (rows, 128), 1)
    pick = base + 2 * block + lane // HEAD_DIM
    return jnp.take_along_axis(per_head, pick, axis=1)


def prep_kernel(x_hbm, raw_ref, log_ref, x_ref, early_ref, late_ref, sem):
    copy = pltpu.make_async_copy(x_hbm, x_ref, sem)
    copy.start()
    raw = raw_ref[...]
    step = jnp.maximum(raw, 0.0) + jnp.log1p(jnp.exp(-jnp.abs(raw)))
    cum = -jnp.exp(log_ref[...]) * step
    row = lax.broadcasted_iota(jnp.int32, (TOK, HEADS), 0)
    shift = 1
    while shift < TOK:
        cum = cum + jnp.where(row >= shift, pltpu.roll(cum, shift, 0), 0.0)
        shift *= 2
    last = cum[TOK - 1 :, :]
    early_ref[:TOK] = jnp.exp(last - cum) * step
    early_ref[TOK:] = jnp.broadcast_to(jnp.exp(last), (8, HEADS))
    late_ref[:TOK] = cum
    late_ref[TOK : 2 * TOK] = cum.T
    late_ref[2 * TOK :] = step.T
    copy.wait()


def prep(conv_input, step_raw, decay_log):
    channels = conv_input.shape[1]
    return pl.pallas_call(
        prep_kernel,
        in_specs=[ANY, VMEM, VMEM],
        out_specs=[VMEM] * 3,
        out_shape=[
            jax.ShapeDtypeStruct((TOK, channels), BF16),
            jax.ShapeDtypeStruct((TOK + 8, HEADS), F32),
            jax.ShapeDtypeStruct((2 * TOK + HEADS, HEADS), F32),
        ],
        scratch_shapes=[pltpu.SemaphoreType.DMA],
        compiler_params=params(),
        cost_estimate=pl.CostEstimate(flops=0, bytes_accessed=0, transcendentals=0),
    )(conv_input, step_raw, decay_log.reshape(1, HEADS))


def convolve(x_ref, edge_ref, w_ref, at):
    cols = pl.ds(pl.multiple_of(at, 128), 128)
    x = x_ref[:, cols].astype(F32)
    edge = edge_ref[:, cols].astype(F32)
    weight = w_ref[:, cols]
    wide = jnp.concatenate([jnp.zeros((8 - KERNEL + 1, 128), F32), edge, x], 0)
    out = None
    for tap in range(KERNEL):
        first = 8 - KERNEL + 1 + tap
        term = wide[first : first + TOK] * weight[tap : tap + 1]
        out = term if out is None else out + term
    return out.astype(BF16)


SLOTS = 4


def convolve_by_loads(x_ref, edge_ref, w_ref, at, wide_ref):
    cols = slice(at, at + 128)
    wide_ref[8 - KERNEL + 1 : 8] = edge_ref[:, cols].astype(F32)
    wide_ref[8:] = x_ref[:, cols].astype(F32)
    out = None
    for tap in range(KERNEL):
        first = 8 - KERNEL + 1 + tap
        term = wide_ref[first : first + TOK] * w_ref[tap : tap + 1, cols]
        out = term if out is None else out + term
    return out.astype(BF16)


def state_kernel(in_ref, edge_ref, w_ref, early_ref, pay_ref, wide_ref):
    factor = early_ref[:TOK]
    decay = early_ref[TOK:]
    blank = jnp.zeros((TAIL - 3 * NBO, 128), F32)
    for group in range(GROUPS):
        writers = convolve_by_loads(in_ref, edge_ref, w_ref, HCOLS + group * STATE, wide_ref.at[0]).astype(F32).T.astype(BF16)
        for owner in range(group * PER // OWN, (group + 1) * PER // OWN):
            base = owner * OWN
            rows = [lanes_of(decay, base, b, 8)[:1] for b in range(NBO)]
            terms = three(jnp.concatenate(rows, 0))
            pay_ref[owner, ROWS:] = jnp.concatenate([*terms, blank], 0).astype(BF16)
            for pair in range(NBO // 2):
                weighted = []
                for b in (2 * pair, 2 * pair + 1):
                    value = convolve_by_loads(
                        in_ref, edge_ref, w_ref, base * HEAD_DIM + b * 128, wide_ref.at[b % SLOTS]
                    )
                    weighted.append((value.astype(F32) * lanes_of(factor, base, b, TOK)).astype(BF16))
                state = jnp.dot(writers, jnp.concatenate(weighted, 1), preferred_element_type=F32)
                for half in range(2):
                    at = (2 * pair + half) * STATE
                    pay_ref[owner, at : at + STATE] = state[:, half * 128 : (half + 1) * 128].astype(BF16)


def states(*args):
    return pl.pallas_call(
        state_kernel,
        in_specs=[VMEM] * 4,
        out_specs=VMEM,
        out_shape=jax.ShapeDtypeStruct((NEAR, PAY, 128), BF16),
        scratch_shapes=[pltpu.VMEM((SLOTS, TOK + 8, 128), F32)],
        compiler_params=params(),
        cost_estimate=pl.CostEstimate(flops=10**8, bytes_accessed=3 * 10**6, transcendentals=0),
    )(*args)


def decays_of(ref, source):
    terms = ref[source, ROWS:].astype(F32)
    return terms[:NBO] + terms[NBO : 2 * NBO] + terms[2 * NBO : 3 * NBO]


def total_kernel(pay_ref, out_ref):
    decays = [decays_of(pay_ref, source) for source in range(NEAR)]
    product = decays[0]
    for decay in decays[1:]:
        product = product * decay
    hi, mid, low = three(product)
    for b in range(NBO):
        rows = slice(b * STATE, (b + 1) * STATE)
        total = pay_ref[0, rows].astype(F32)
        for source in range(1, NEAR):
            total = decays[source][b : b + 1] * total + pay_ref[source, rows].astype(F32)
        tail = jnp.concatenate(
            [hi[b : b + 1], mid[b : b + 1], low[b : b + 1], jnp.zeros((5, 128), F32)], 0
        )
        for part in range(STATE // SROWS):
            share = jnp.concatenate([total[part * SROWS : (part + 1) * SROWS], tail], 0)
            out_ref[b * (STATE // SROWS) + part] = share.astype(BF16)


def row_total(pays):
    return pl.pallas_call(
        total_kernel,
        in_specs=[VMEM],
        out_specs=VMEM,
        out_shape=jax.ShapeDtypeStruct((SHARES, TROWS, 128), BF16),
        compiler_params=params(),
    )(pays)


def row_of(rows_ref, at):
    block = rows_ref[at].astype(F32)
    tail = block[SROWS:]
    return block[:SROWS], tail[:1] + tail[1:2] + tail[2:3]


def group_kernel(rows_ref, out_ref):
    for y in range(NY):
        total, product = row_of(rows_ref, y * NZH)
        for z in range(1, NZH):
            state, decay = row_of(rows_ref, y * NZH + z)
            total = decay * total + state
            product = decay * product
        out_ref[y, :SROWS] = total
        out_ref[y, SROWS:] = jnp.broadcast_to(product, (8, 128))


def group_total(rows):
    return pl.pallas_call(
        group_kernel,
        in_specs=[VMEM],
        out_specs=VMEM,
        out_shape=jax.ShapeDtypeStruct((NY, TROWS, 128), F32),
        compiler_params=params(),
    )(rows)


def scan_kernel(core_ref, rows_ref, own_ref, other_ref, out_ref):
    first = core_ref[0] == 0
    entry = jnp.zeros((SROWS, 128), F32)
    for y in range(NY):
        own, other = own_ref[y], other_ref[y]
        one = jnp.where(first, own, other)
        two = jnp.where(first, other, own)
        middle = one[SROWS : SROWS + 1] * entry + one[:SROWS]
        state = jnp.where(first, entry, middle)
        entry = two[SROWS : SROWS + 1] * middle + two[:SROWS]
        for z in range(NZH):
            out_ref[y * NZH + z] = state.astype(BF16)
            if z < NZH - 1:
                term, decay = row_of(rows_ref, y * NZH + z)
                state = decay * state + term


def scan(core, rows, own, other):
    return pl.pallas_call(
        scan_kernel,
        in_specs=[SMEM] + [VMEM] * 3,
        out_specs=VMEM,
        out_shape=jax.ShapeDtypeStruct((SHARES, SROWS, 128), BF16),
        compiler_params=params(),
    )(core, rows, own, other)


def enter_kernel(entry_ref, pay_ref, out_ref):
    decays = [decays_of(pay_ref, source) for source in range(NEAR - 1)]
    for b in range(NBO):
        rows = slice(b * STATE, (b + 1) * STATE)
        state = entry_ref[rows].astype(F32)
        for target in range(NEAR):
            out_ref[target, rows] = state.astype(BF16)
            if target < NEAR - 1:
                state = decays[target][b : b + 1] * state + pay_ref[target, rows].astype(F32)


def enter(entry, pays):
    return pl.pallas_call(
        enter_kernel,
        in_specs=[VMEM] * 2,
        out_specs=VMEM,
        out_shape=jax.ShapeDtypeStruct((NEAR, ROWS, 128), BF16),
        compiler_params=params(),
    )(entry, pays)


def local_kernel(in_ref, edge_ref, w_ref, late_ref, gain_ref, out_ref, rea_ref, wide_ref):
    cum = late_ref[:TOK]
    gain = jnp.broadcast_to(gain_ref[...], (8, HEADS))
    row = lax.broadcasted_iota(jnp.int32, (TOK, TOK), 0)
    col = lax.broadcasted_iota(jnp.int32, (TOK, TOK), 1)
    causal = row >= col
    first = col < HEAD_DIM
    for group in range(GROUPS):
        base = group * PER
        writers = convolve_by_loads(in_ref, edge_ref, w_ref, HCOLS + group * STATE, wide_ref.at[0])
        readers = convolve_by_loads(
            in_ref, edge_ref, w_ref, HCOLS + (GROUPS + group) * STATE, wide_ref.at[1]
        )
        rea_ref[:, group * STATE : (group + 1) * STATE] = readers
        affinity = lax.dot_general(
            readers, writers, (((1,), (1,)), ((), ())), preferred_element_type=F32
        )
        cum_t = late_ref[TOK + base : TOK + base + PER]
        step_t = late_ref[TOK + HEADS + base : TOK + HEADS + base + PER]
        for b in range(NB):
            scores = []
            for h in (2 * b, 2 * b + 1):
                here = jnp.take_along_axis(cum, jnp.full((TOK, TOK), base + h, jnp.int32), axis=1)
                span = jnp.where(causal, here - cum_t[h : h + 1], -1e30)
                weight = jnp.exp(span) * step_t[h : h + 1]
                scores.append((weight * affinity).astype(BF16))
            at = base * HEAD_DIM + b * 128
            value = convolve_by_loads(in_ref, edge_ref, w_ref, at, wide_ref.at[b % SLOTS])
            zero = jnp.zeros_like(value)
            apart = jnp.concatenate([jnp.where(first, value, zero), jnp.where(first, zero, value)], 0)
            local = jnp.dot(jnp.concatenate(scores, 1), apart, preferred_element_type=F32)
            skip = lanes_of(gain, base, b, 8)[:1]
            out_ref[:, at : at + 128] = local + skip * value.astype(F32)


def local(*args):
    return pl.pallas_call(
        local_kernel,
        in_specs=[VMEM] * 5,
        out_specs=[VMEM] * 2,
        out_shape=[
            jax.ShapeDtypeStruct((TOK, HCOLS), F32),
            jax.ShapeDtypeStruct((TOK, GROUPS * STATE), BF16),
        ],
        scratch_shapes=[pltpu.VMEM((SLOTS, TOK + 8, 128), F32)],
        compiler_params=params(),
        cost_estimate=pl.CostEstimate(flops=10**9, bytes_accessed=8 * 10**6, transcendentals=0),
    )(*args)


def final_kernel(rea_ref, late_ref, part_ref, state_ref, out_ref, buf, sems):
    growth = jnp.exp(late_ref[:TOK])
    width = OWN * HEAD_DIM
    copies = []
    for owner in range(NEAR):
        base = owner * OWN
        group = base // PER
        readers = rea_ref[:, group * STATE : (group + 1) * STATE]
        for pair in range(NBO // 2):
            at = 2 * pair * STATE
            both = jnp.concatenate(
                [state_ref[owner, at : at + STATE], state_ref[owner, at + STATE : at + 2 * STATE]], 1
            )
            carried = jnp.dot(readers, both, preferred_element_type=F32)
            for half in range(2):
                b = 2 * pair + half
                cols = slice(owner * width + b * 128, owner * width + (b + 1) * 128)
                grow = lanes_of(growth, base, b, TOK)
                result = part_ref[:, cols] + carried[:, half * 128 : (half + 1) * 128] * grow
                buf[:, cols] = result.astype(BF16)
        cols = pl.ds(owner * width, width)
        copies.append(pltpu.make_async_copy(buf.at[:, cols], out_ref.at[:, cols], sems.at[owner]))
        copies[-1].start()
    for copy in copies:
        copy.wait()


def final(*args):
    return pl.pallas_call(
        final_kernel,
        in_specs=[VMEM] * 4,
        out_specs=ANY,
        out_shape=jax.ShapeDtypeStruct((TOK, HCOLS), BF16),
        scratch_shapes=[pltpu.VMEM((TOK, HCOLS), BF16), pltpu.SemaphoreType.DMA((NEAR,))],
        compiler_params=params(),
        cost_estimate=pl.CostEstimate(flops=10**8, bytes_accessed=2 * 10**6, transcendentals=0),
    )(*args)


def body(conv_input, conv_weight, step_raw, decay_log, skip_gain):
    count = lax.axis_size(AXES)
    core = lax.axis_index("core").reshape(1)
    edge = lax.ppermute(conv_input[TOK - KERNEL + 1 :], AXES, [(i, i + 1) for i in range(count - 1)])
    held, early, late = prep(conv_input, step_raw, decay_log)
    made = states(held, edge, conv_weight, early)
    pays = lax.all_to_all(made, NEAR_AXES, 0, 0, tiled=True)
    late, pays = lax.optimization_barrier((late, pays))
    rows = lax.all_to_all(row_total(pays), FAR_AXES, 0, 0, tiled=True)
    part, readers = local(conv_input, edge, conv_weight, late, skip_gain.reshape(1, HEADS))
    rows, part, readers = lax.optimization_barrier((rows, part, readers))
    own = group_total(rows)
    other = lax.ppermute(own, "core", [(0, 1), (1, 0)])
    entry = lax.all_to_all(scan(core, rows, own, other), FAR_AXES, 0, 0, tiled=True)
    entering = enter(entry.reshape(ROWS, 128), pays)
    state = lax.all_to_all(entering, NEAR_AXES, 0, 0, tiled=True)
    return final(readers, late, part, state)


def solution(mesh):
    fine = Mesh(mesh.devices.reshape(NY, 2, NZH, NZL, NX), AXES)
    in_specs = (P(AXES, None), P(), P(AXES, None), P(), P())
    return jax.shard_map(body, mesh=fine, in_specs=in_specs, out_specs=P(AXES, None), check_vma=False)
```
